256 devices in a mesh: tile: 32 (over x_lo, z, core), src: 8 (over y, x_hi).
Axes of the slice: x: 4 (x_hi: 2, x_lo: 2; x = x_hi * 2 + x_lo), y: 4, z: 8, core: 2. Of those that a mesh axis runs over, the one named last changes fastest.
Arguments:
- mask: float32 [32, 512, 512], P('tile'), may hold values from 0 to 1.2, as said below
- target: int32 [32, 512, 512], P('tile'), may hold values 0 or 1
- shifts: int32 [64, 2], P('src'), may hold values from -32 to 32
- source_weights: float32 [64], P('src'), may hold values from 0.5 to 4
- pupil: int32 [128, 128], replicated, may hold values from 0 to 1, as said below
Outputs:
- new_mask: float32 [32, 512, 512], P('tile')
- new_weights: float32 [64], P('src')
- resist: float32 [32, 512, 512], P('tile')
The draws below stay inside these ranges and needn't reach their ends.
Inputs may be any that keep to these rules, and one draw needn't show every extreme that they name: `mask`: non-negative transmissions. `pupil`: row i (frequency f_i = i - 64) is 1 where f_i^2 + f_j^2 <= R_i^2 and 0 elsewhere, with a radius R_i of 48 to 64 for each row.
All inputs are finite; a program needn't handle non-finite values. No bound on the sum of `target` on one device may be relied on, other than what follows from the above.
Results may differ from the reference program's by a relative error of at most 0.017.
The reference program's roundings to bfloat16 on the way count: a program that leaves them out, or rounds other values in their place, can miss the bound.
Values may be sent and summed in bfloat16 or wider, within the bound.
No kernel may reach another device: no remote copies, remote signals or barrier semaphores. Data moves between devices by JAX's collectives and lax.ppermute only.
A program may use at most 128 MiB of HBM per device.

```python
import math
import jax
import jax.numpy as jnp
from jax import lax

TS = 512
HALO = 64
BAND = 128
SHIFT_MAX = 32
GRID_ROWS = 4
NE = 640
SRC = 64
TILES = 32
GRID_COLS = 8
PIXELS = 8388608


def draw_mask(key, part):
    key = jax.random.fold_in(key, 11)
    uniform_part = jax.random.uniform(key, (TILES, TS, TS), jnp.float32)
    levels = 0.4 * 3.0 ** (jnp.arange(TILES, dtype=jnp.float32) / max(TILES - 1, 1))
    values = uniform_part
    return levels[:, None, None] * values


def draw_pupil(key, part):
    key = jax.random.fold_in(key, 12)
    radii = jax.random.randint(key, (BAND,), 3 * BAND // 8, BAND // 2 + 1)
    freq_index = jnp.arange(BAND, dtype=jnp.int32) - BAND // 2
    squared = freq_index[:, None] * freq_index[:, None] + freq_index[None, :] * freq_index[None, :]
    return (squared <= radii[:, None] * radii[:, None]).astype(jnp.int32)


def plant(result, stream_key, least, high):
    spot = [jax.random.randint(jax.random.fold_in(stream_key, axis), (), 0, length) for axis, length in enumerate(result.shape)]
    widest = result.shape.index(max(result.shape))
    next_to = spot[:widest] + [(spot[widest] + 1) % result.shape[widest]] + spot[widest + 1:]
    return result.at[tuple(spot)].set(least).at[tuple(next_to)].set(high)


def steps_of(own_key, shape, shards, low, high):
    gain, own = 1.0, jax.random.fold_in(own_key, 6)
    for axis_at, shards_of in shards:
        heights = jnp.exp(jax.random.uniform(jax.random.fold_in(own, axis_at), (shards_of,), jnp.float32, low / len(shards), high / len(shards)))
        gain = gain * jnp.repeat(heights, shape[axis_at] // shards_of).reshape([-1 if axis == axis_at else 1 for axis in range(len(shape))])
    return gain


def setup_inputs(seed: int = 0) -> dict:
    arg_keys = jax.random.split(jax.random.key(seed), 6)
    return {
        "mask": draw_mask(jax.random.fold_in(arg_keys[5], 71), 0),
        "target": plant((jax.random.randint(arg_keys[1], (TILES, TS, TS), 0, 2) < 1).astype(jnp.int32), jax.random.fold_in(arg_keys[1], 1), 0, 1),
        "shifts": plant(jax.random.randint(arg_keys[2], (SRC, 2), -SHIFT_MAX, SHIFT_MAX + 1), jax.random.fold_in(arg_keys[2], 1), -SHIFT_MAX, SHIFT_MAX).astype(jnp.int32),
        "source_weights": jnp.clip(jnp.exp(math.log(4.0) - 2.0794415 * jax.random.uniform(arg_keys[3], (SRC,), jnp.float32) ** steps_of(arg_keys[3], (SRC,), ((0, 8),), -0.2, 0.2)), 0.5, 4.0),
        "pupil": draw_pupil(jax.random.fold_in(arg_keys[5], 71), 0),
    }


steepness = 10.0
threshold = 0.25
mask_rate = 0.5
source_rate = 8.0


def make_tables(tile_size, band_width):
    extent = tile_size + 2 * HALO
    spectrum_span = band_width + 2 * SHIFT_MAX
    freq_index = jnp.arange(spectrum_span, dtype=jnp.int32) - spectrum_span // 2
    positions = jnp.arange(extent, dtype=jnp.int32)
    phases = jnp.mod(freq_index[:, None] * positions[None, :], extent).astype(jnp.float32) * (2.0 * math.pi / extent)
    freq_re = (jnp.cos(phases) / extent).astype(jnp.bfloat16)
    freq_im = (-jnp.sin(phases) / extent).astype(jnp.bfloat16)
    band_index = jnp.arange(band_width, dtype=jnp.int32) - band_width // 2
    pixel_ext = jnp.arange(tile_size, dtype=jnp.int32) + HALO
    back_phase = jnp.mod(pixel_ext[:, None] * band_index[None, :], extent).astype(jnp.float32) * (2.0 * math.pi / extent)
    back_re = jnp.cos(back_phase).astype(jnp.bfloat16)
    back_im = jnp.sin(back_phase).astype(jnp.bfloat16)
    return freq_re, freq_im, back_re, back_im


def dot_nn(left, right):
    return jnp.dot(left, right, preferred_element_type=jnp.float32)


def dot_nt(left, right):
    return lax.dot_general(left, right, (((1,), (1,)), ((), ())), preferred_element_type=jnp.float32)


def dot_tn(left, right):
    return lax.dot_general(left, right, (((0,), (0,)), ((), ())), preferred_element_type=jnp.float32)


def spectrum_rows(ext_bf, freq_re, freq_im, rows_re, rows_im):
    prod_re = dot_nn(rows_re, ext_bf).astype(jnp.bfloat16)
    prod_im = dot_nn(rows_im, ext_bf).astype(jnp.bfloat16)
    spec_re = dot_nt(prod_re, freq_re) - dot_nt(prod_im, freq_im)
    spec_im = dot_nt(prod_re, freq_im) + dot_nt(prod_im, freq_re)
    return spec_re, spec_im


def source_field(spec_re, spec_im, source_shift, pupil_gain, left_re, left_im, back_re, back_im):
    band_width = pupil_gain.shape[0]
    offsets = (SHIFT_MAX - source_shift).astype(jnp.int32)
    win_re = (lax.dynamic_slice(spec_re, (offsets[0], offsets[1]), (band_width, band_width)) * pupil_gain).astype(jnp.bfloat16)
    win_im = (lax.dynamic_slice(spec_im, (offsets[0], offsets[1]), (band_width, band_width)) * pupil_gain).astype(jnp.bfloat16)
    amp_re = (dot_nn(left_re, win_re) - dot_nn(left_im, win_im)).astype(jnp.bfloat16)
    amp_im = (dot_nn(left_re, win_im) + dot_nn(left_im, win_re)).astype(jnp.bfloat16)
    field_re = dot_nt(amp_re, back_re) - dot_nt(amp_im, back_im)
    field_im = dot_nt(amp_re, back_im) + dot_nt(amp_im, back_re)
    return field_re, field_im


def source_adjoint(grad_re, grad_im, source_shift, coef_map, field_re, field_im, pupil_gain, left_re, left_im, back_re, back_im):
    band_width = pupil_gain.shape[0]
    dfield_re = (coef_map * field_re).astype(jnp.bfloat16)
    dfield_im = (coef_map * field_im).astype(jnp.bfloat16)
    damp_re = (dot_nn(dfield_re, back_re) + dot_nn(dfield_im, back_im)).astype(jnp.bfloat16)
    damp_im = (dot_nn(dfield_im, back_re) - dot_nn(dfield_re, back_im)).astype(jnp.bfloat16)
    dwin_re = (dot_tn(left_re, damp_re) + dot_tn(left_im, damp_im)) * pupil_gain
    dwin_im = (dot_tn(left_re, damp_im) - dot_tn(left_im, damp_re)) * pupil_gain
    offsets = (SHIFT_MAX - source_shift).astype(jnp.int32)
    corner = (offsets[0], offsets[1])
    grad_re = lax.dynamic_update_slice(grad_re, lax.dynamic_slice(grad_re, corner, (band_width, band_width)) + dwin_re, corner)
    grad_im = lax.dynamic_update_slice(grad_im, lax.dynamic_slice(grad_im, corner, (band_width, band_width)) + dwin_im, corner)
    return grad_re, grad_im


def mask_adjoint(grad_re, grad_im, freq_re, freq_im):
    highest = lax.Precision.HIGHEST
    wide_re = freq_re.astype(jnp.float32)
    wide_im = freq_im.astype(jnp.float32)
    dprod_re = jnp.dot(grad_re, wide_re, precision=highest) + jnp.dot(grad_im, wide_im, precision=highest)
    dprod_im = jnp.dot(grad_im, wide_re, precision=highest) - jnp.dot(grad_re, wide_im, precision=highest)
    first_term = lax.dot_general(wide_re, dprod_re, (((0,), (0,)), ((), ())), precision=highest)
    second_term = lax.dot_general(wide_im, dprod_im, (((0,), (0,)), ((), ())), precision=highest)
    return first_term + second_term


def tile_step(ext_bf, target_tile, shifts, source_weights, pupil_gain, tables, sources):
    freq_re, freq_im, back_re, back_im = tables
    spec_re, spec_im = spectrum_rows(ext_bf, freq_re, freq_im, freq_re, freq_im)

    def forward(totals, source_item):
        source_shift, source_weight = source_item
        field_re, field_im = source_field(spec_re, spec_im, source_shift, pupil_gain, back_re, back_im, back_re, back_im)
        intensity = field_re * field_re + field_im * field_im
        return totals + source_weight * intensity, (field_re, field_im)

    zero_image = jnp.zeros(target_tile.shape, jnp.float32)
    partial_image, (fields_re, fields_im) = lax.scan(forward, zero_image, (shifts, source_weights))
    return partial_image, fields_re, fields_im, spec_re.shape[0]


def tile_backward(aerial, target_tile, shifts, source_weights, fields_re, fields_im, pupil_gain, tables, sources, spectrum_span):
    freq_re, freq_im, back_re, back_im = tables
    resist_tile = jax.nn.sigmoid(steepness * (aerial - threshold))
    grad_img = 2.0 * (resist_tile - target_tile.astype(jnp.float32)) * resist_tile * (1.0 - resist_tile) * steepness

    def backward(totals, source_item):
        source_shift, source_weight, field_re, field_im = source_item
        coef_map = (2.0 * source_weight / sources) * grad_img
        grad_re, grad_im = source_adjoint(totals[0], totals[1], source_shift, coef_map, field_re, field_im, pupil_gain, back_re, back_im, back_re, back_im)
        weight_term = jnp.sum(grad_img * (field_re * field_re + field_im * field_im))
        return (grad_re, grad_im), weight_term

    zero_spec = jnp.zeros((spectrum_span, spectrum_span), jnp.float32)
    (grad_re, grad_im), weight_terms = lax.scan(backward, (zero_spec, zero_spec), (shifts, source_weights, fields_re, fields_im))
    return resist_tile, grad_re, grad_im, weight_terms


def reference(mask, target, shifts, source_weights, pupil):
    tables = make_tables(TS, BAND)
    freq_re, freq_im = tables[0], tables[1]
    pupil_gain = pupil.astype(jnp.float32)
    whole = mask.astype(jnp.bfloat16).reshape(GRID_ROWS, GRID_COLS, TS, TS).transpose(0, 2, 1, 3).reshape(GRID_ROWS * TS, GRID_COLS * TS)
    padded = jnp.pad(whole, HALO)

    def per_tile(position):
        grid_row = position // GRID_COLS
        grid_col = position % GRID_COLS
        ext_bf = lax.dynamic_slice(padded, (grid_row * TS, grid_col * TS), (NE, NE))
        target_tile = target[position]
        partial_image, fields_re, fields_im, spectrum_span = tile_step(ext_bf, target_tile, shifts, source_weights, pupil_gain, tables, SRC)
        aerial = partial_image / SRC
        resist_tile, grad_re, grad_im, weight_terms = tile_backward(aerial, target_tile, shifts, source_weights, fields_re, fields_im, pupil_gain, tables, SRC, spectrum_span)
        ext_grad = mask_adjoint(grad_re, grad_im, freq_re, freq_im)
        return resist_tile, ext_grad, weight_terms

    resist, ext_grads, weight_terms = lax.map(per_tile, jnp.arange(TILES, dtype=jnp.int32))

    def place(position, totals):
        grid_row = position // GRID_COLS
        grid_col = position % GRID_COLS
        corner = (grid_row * TS, grid_col * TS)
        region = lax.dynamic_slice(totals, corner, (NE, NE)) + ext_grads[position]
        return lax.dynamic_update_slice(totals, region, corner)

    totals = jnp.zeros((GRID_ROWS * TS + 2 * HALO, GRID_COLS * TS + 2 * HALO), jnp.float32)
    totals = lax.fori_loop(0, TILES, place, totals)
    cropped = totals[HALO:HALO + GRID_ROWS * TS, HALO:HALO + GRID_COLS * TS]
    tile_grads = cropped.reshape(GRID_ROWS, TS, GRID_COLS, TS).transpose(0, 2, 1, 3).reshape(TILES, TS, TS)
    new_mask = mask - mask_rate * tile_grads
    new_weights = source_weights - source_rate * jnp.sum(weight_terms, axis=0) / PIXELS
    return new_mask, new_weights, resist
```

```python
import math

import jax
import jax.numpy as jnp
import ml_dtypes
import numpy as np
from jax import lax
from jax.experimental import pallas as pl
from jax.experimental.pallas import tpu as pltpu
from jax.sharding import PartitionSpec as P

TS = 512
HALO = 64
BAND = 128
SHIFT_MAX = 32
GRID_ROWS = 4
NE = TS + 2 * HALO
SPAN = BAND + 2 * SHIFT_MAX
HALF = 256
BATCH = 4

steepness = 10.0
threshold = 0.25
mask_rate = 0.5
source_rate = 8.0

BF = jnp.bfloat16
F32 = jnp.float32

ORDER = np.concatenate([np.arange(HALO, HALO + TS), np.arange(HALO), np.arange(HALO + TS, NE)])


def make_tables():
    freq_index = np.arange(SPAN) - SPAN // 2
    phases = np.mod(freq_index[:, None] * ORDER[None, :], NE) * (2.0 * math.pi / NE)
    freq_re, freq_im = np.cos(phases) / NE, -np.sin(phases) / NE
    band_index = np.arange(BAND) - BAND // 2
    back_phase = np.mod((np.arange(TS) + HALO)[:, None] * band_index[None, :], NE) * (2.0 * math.pi / NE)
    back_re, back_im = np.cos(back_phase), np.sin(back_phase)

    def bf(table):
        return np.ascontiguousarray(table).astype(np.float32).astype(ml_dtypes.bfloat16)

    freq = np.concatenate([freq_re, freq_im], 0)
    gap = np.zeros((NE, HALF - SPAN))
    to_re = np.concatenate([freq_re.T, gap, freq_im.T, gap], 1)
    to_im = np.concatenate([-freq_im.T, gap, freq_re.T, gap], 1)
    back_t = np.block([[back_re.T, back_im.T], [-back_im.T, back_re.T]])
    rows = np.concatenate([back_re, back_im], 1)
    return tuple(bf(t) for t in (freq, to_re, to_im, back_t, back_t.T, rows, freq.T))


def rows_t_table(blocks):
    rows = make_tables()[5]
    step = TS // blocks
    parts = [
        np.concatenate([rows[i * step : (i + 1) * step, :BAND].T, rows[i * step : (i + 1) * step, BAND:].T], 1)
        for i in range(blocks)
    ]
    return np.stack(parts)


def dot(left, right):
    return lax.dot_general(left, right, (((1,), (0,)), ((), ())), preferred_element_type=F32)


def dot_nt(left, right):
    return lax.dot_general(left, right, (((1,), (1,)), ((), ())), preferred_element_type=F32)


def source_kernel(
    place, shift, weight, mask, vert_1, vert_2, side_1, side_2, target, pupil,
    freq, to_re, to_im, back_t, back, rows, rows_t,
    dspec_out, resist_out, weight_out,
    spec, fields, image, dspec, terms, bits, sem,
):
    step = resist_out.shape[0]
    k, row_odd, col_odd = place[0], place[1] == 1, place[2] == 1
    fetch = pltpu.make_async_copy(target.at[0, pl.ds(pl.multiple_of(k * step, step), step), :], bits, sem)
    fetch.start()

    v1, v2 = vert_1[...].astype(F32), vert_2[...].astype(F32)
    halo_rows = jnp.concatenate([jnp.where(row_odd, v1, v2), jnp.where(row_odd, v2, v1)], 0).astype(BF)
    s1, s2 = side_1[...].astype(F32), side_2[...].astype(F32)
    left, right = jnp.where(col_odd, s1, s2), jnp.where(col_odd, s2, s1)
    first = lax.broadcasted_iota(jnp.int32, left.shape, 1) < HALO
    halo_cols = jnp.concatenate(
        [jnp.where(first, left, pltpu.roll(right, HALO, 1)), jnp.where(first, pltpu.roll(left, HALO, 1), right)], 0
    ).astype(BF)
    prod_mid = dot(freq[:, :TS], mask[0].astype(BF)) + dot(freq[:, TS:], halo_rows)
    prod_side = dot(freq[...], halo_cols)
    prod = jnp.concatenate([prod_mid, prod_side], 1).astype(BF)
    whole = dot(prod[:SPAN], to_re[...]) + dot(prod[SPAN:], to_im[...])
    for j in range(4):
        spec[j] = whole[:, j * 128 : (j + 1) * 128]

    gain = pupil[...].astype(F32)
    own_rows = rows[pl.ds(pl.multiple_of(k * step, step), step), :]
    sources = shift.shape[0] * BATCH * 2
    image[...] = jnp.zeros_like(image)
    dspec[...] = jnp.zeros_like(dspec)
    terms[...] = jnp.zeros_like(terms)

    def where_of(s):
        return SHIFT_MAX - shift[s // 8, s % 8], SHIFT_MAX - shift[s // 8, 8 + s % 8], weight[s // 8, s % 8]

    def forward(i, _):
        amps = []
        for u in range(BATCH):
            down, over, _w = where_of(i * BATCH + u)
            band = [spec[j, pl.ds(down, BAND), :] for j in range(4)]
            turn = lax.bitwise_and(HALF - over, HALF - 1)
            win_re = pltpu.roll(jnp.concatenate(band[:2], 1), turn, 1)[:, :BAND] * gain
            win_im = pltpu.roll(jnp.concatenate(band[2:], 1), turn, 1)[:, :BAND] * gain
            window = jnp.concatenate(
                [jnp.concatenate([win_re, win_im], 1), jnp.concatenate([-win_im, win_re], 1)], 0
            ).astype(BF)
            amps.append(dot(own_rows, window).astype(BF))
        field = dot(jnp.concatenate(amps, 0), back_t[...])
        fields[pl.ds(pl.multiple_of(i * (BATCH * step), BATCH * step), BATCH * step), :] = field
        total = image[...]
        for u in range(BATCH):
            _d, _o, w = where_of(i * BATCH + u)
            part = field[u * step : (u + 1) * step]
            total = total + w * (part[:, :TS] * part[:, :TS] + part[:, TS:] * part[:, TS:])
        image[...] = total
        return 0

    lax.fori_loop(0, sources // BATCH, forward, 0)

    fetch.wait()
    resist = jax.nn.sigmoid(steepness * (image[...] * (1.0 / sources) - threshold))
    resist_out[...] = resist.astype(BF)
    image[...] = 2.0 * (resist - bits[...].astype(F32)) * resist * (1.0 - resist) * steepness

    rows_turned = rows_t[k]

    def backward(i, _):
        dfields = []
        grad = image[...]
        for u in range(BATCH):
            s = i * BATCH + u
            _d, _o, w = where_of(s)
            at = pl.ds(pl.multiple_of(i * (BATCH * step) + u * step, step), step)
            field_re, field_im = fields[at, :TS], fields[at, TS:]
            term = jnp.sum(grad * (field_re * field_re + field_im * field_im), 0, keepdims=True)
            terms[pl.ds(s, 1), :] = term[:, :128] + term[:, 128:256] + term[:, 256:384] + term[:, 384:]
            coef = (2.0 * w / sources) * grad
            dfields.append(jnp.concatenate([coef * field_re, coef * field_im], 1).astype(BF))
        damp = dot(jnp.concatenate(dfields, 0), back[...])
        for u in range(BATCH):
            down, over, _w = where_of(i * BATCH + u)
            part = damp[u * step : (u + 1) * step]
            damp_re, damp_im = part[:, :BAND], part[:, BAND:]
            pair = jnp.concatenate(
                [jnp.concatenate([damp_re, damp_im], 1), jnp.concatenate([damp_im, -damp_re], 1)], 0
            ).astype(BF)
            dwin = dot(rows_turned, pair)
            empty = jnp.zeros((BAND, HALF - BAND), F32)
            dwin_re = pltpu.roll(jnp.concatenate([dwin[:, :BAND] * gain, empty], 1), over, 1)
            dwin_im = pltpu.roll(jnp.concatenate([dwin[:, BAND:] * gain, empty], 1), over, 1)
            for j, piece in enumerate((dwin_re[:, :128], dwin_re[:, 128:], dwin_im[:, :128], dwin_im[:, 128:])):
                dspec[j, pl.ds(down, BAND), :] += piece
        return 0

    lax.fori_loop(0, sources // BATCH, backward, 0)
    for j in range(4):
        dspec_out[:, j * 128 : (j + 1) * 128] = dspec[j].astype(BF)
    weight_out[...] = lax.dot_general(
        jnp.ones((8, 128), F32), terms[...], (((1,), (1,)), ((), ())),
        precision=lax.Precision.HIGHEST, preferred_element_type=F32,
    )


def split(values):
    high = values.astype(BF)
    return high, (values - high.astype(F32)).astype(BF)


def mask_kernel(place, mask, part_1, part_2, to_re, to_im, freq_t, base_out, vert_1, vert_2, sides_out):
    row_odd = place[1] == 1
    high, low = split(part_1[...].astype(F32) + part_2[...].astype(F32))
    both = jnp.concatenate([high, low], 0)
    prod_re, prod_im = dot_nt(both, to_re[...]), dot_nt(both, to_im[...])
    prod = jnp.concatenate([prod_re[:SPAN] + prod_re[SPAN:], prod_im[:SPAN] + prod_im[SPAN:]], 0)
    high, low = split(prod)
    ext = dot(freq_t[...], high) + dot(freq_t[...], low)
    base_out[...] = mask[0] - mask_rate * ext[:TS, :TS]
    sides_out[...] = ext[:TS, TS:]
    above, below = ext[TS : TS + HALO], ext[TS + HALO :]
    vert_1[...] = jnp.where(row_odd, above, below).astype(BF)
    vert_2[...] = jnp.where(row_odd, below, above).astype(BF)


def side_kernel(place, sides, got_1, got_2, side_1, side_2, work):
    row_odd, col_odd = place[1] == 1, place[2] == 1
    g1, g2 = got_1[:, TS:].astype(F32), got_2[:, TS:].astype(F32)
    work[...] = sides[...]
    work[:HALO] += jnp.where(row_odd, g1, g2)
    work[TS - HALO :] += jnp.where(row_odd, g2, g1)
    upper, lower = work[: TS // 2], work[TS // 2 :]
    first = lax.broadcasted_iota(jnp.int32, upper.shape, 1) < HALO
    left = jnp.where(first, upper, pltpu.roll(lower, HALO, 1))
    right = jnp.where(first, pltpu.roll(upper, HALO, 1), lower)
    side_1[...] = jnp.where(col_odd, left, right).astype(BF)
    side_2[...] = jnp.where(col_odd, right, left).astype(BF)


def final_kernel(place, base, got_1, got_2, side_1, side_2, *rest):
    pieces, (mask_out, resist_out) = rest[:-2], rest[-2:]
    k, row_odd, col_odd = place[0], place[1] == 1, place[2] == 1
    step = pieces[0].shape[0]
    for m, piece in enumerate(pieces):
        at = lax.bitwise_xor(k, m)
        resist_out[0, pl.ds(pl.multiple_of(at * step, step), step), :] = piece[...].astype(F32)
    g1, g2 = got_1[:, :TS].astype(F32), got_2[:, :TS].astype(F32)
    mask_out[0] = base[...]
    mask_out[0, :HALO, :] -= mask_rate * jnp.where(row_odd, g1, g2)
    mask_out[0, TS - HALO :, :] -= mask_rate * jnp.where(row_odd, g2, g1)
    s1, s2 = side_1[...].astype(F32), side_2[...].astype(F32)
    left, right = jnp.where(col_odd, s1, s2), jnp.where(col_odd, s2, s1)
    first = lax.broadcasted_iota(jnp.int32, left.shape, 1) < HALO
    half = TS // 2
    mask_out[0, :half, :128] -= mask_rate * jnp.where(first, left, 0.0)
    mask_out[0, half:, :128] -= mask_rate * jnp.where(first, pltpu.roll(left, HALO, 1), 0.0)
    mask_out[0, :half, TS - 128 :] -= mask_rate * jnp.where(first, 0.0, pltpu.roll(right, HALO, 1))
    mask_out[0, half:, TS - 128 :] -= mask_rate * jnp.where(first, 0.0, right)


SMEM = pl.BlockSpec(memory_space=pltpu.SMEM)
VMEM = pl.BlockSpec(memory_space=pltpu.VMEM)
HBM = pl.BlockSpec(memory_space=pl.ANY)


def shaped(shape, dtype):
    return jax.ShapeDtypeStruct(shape, dtype)


def grid_routes(tiles, columns):
    row_swap = [(t, t ^ columns) for t in range(tiles)]
    row_next = [(t, t + columns) for t in range(tiles) if (t // columns) % 2 == 1 and t + columns < tiles]
    col_swap = [(t, t ^ 1) for t in range(tiles)]
    col_next = [(t, t + 1) for t in range(tiles) if t % 2 == 1 and (t + 1) % columns != 0]
    back = lambda route: route + [(b, a) for a, b in route]
    return row_swap, back(row_next), col_swap, back(col_next)


def src_swap(block, distance, count):
    return lax.ppermute(block, "src", [(i, i ^ distance) for i in range(count)])


def tile_swap(block, distance, count):
    return lax.ppermute(block, "tile", [(i, i ^ distance) for i in range(count)])


def per_device(mask, target, shifts, source_weights, pupil):
    tiles, groups = lax.axis_size("tile"), lax.axis_size("src")
    columns = tiles // GRID_ROWS
    tile, k = lax.axis_index("tile"), lax.axis_index("src")
    row_odd, col_odd = (tile // columns) % 2 == 1, tile % 2 == 1
    place = jnp.stack([k, row_odd.astype(jnp.int32), col_odd.astype(jnp.int32)]).astype(jnp.int32)
    row_swap, row_next, col_swap, col_next = grid_routes(tiles, columns)
    freq, to_re, to_im, back_t, back, rows, freq_t = (jnp.asarray(t) for t in make_tables())
    rows_t = jnp.asarray(rows_t_table(groups))
    own = shifts.shape[0]
    step = TS // groups

    line = jnp.concatenate([shifts[:, 0].astype(F32), shifts[:, 1].astype(F32), source_weights])
    line = jnp.pad(line, (0, 128 - line.shape[0]))
    info = jnp.where(jnp.arange(groups)[:, None] == k, line[None, :], 0.0)
    for distance in (1, 2, 4):
        info = info + src_swap(info, distance, groups)
    all_shifts = info[:, : 2 * own].astype(jnp.int32)
    all_weights = info[:, 2 * own : 3 * own]

    top, bottom = mask[0, :HALO].astype(BF), mask[0, TS - HALO :].astype(BF)
    vert_1 = lax.ppermute(jnp.where(row_odd, top, bottom), "tile", row_swap)
    vert_2 = lax.ppermute(jnp.where(row_odd, bottom, top), "tile", row_next)
    above, below = jnp.where(row_odd, vert_1, vert_2), jnp.where(row_odd, vert_2, vert_1)

    def packed(cols):
        edge = jnp.concatenate([mask[0][:, cols].astype(BF), above[:, cols], below[:, cols]], 0)
        return jnp.concatenate([edge[: NE // 2], edge[NE // 2 :]], 1)

    left, right = packed(slice(0, HALO)), packed(slice(TS - HALO, TS))
    side_1 = lax.ppermute(jnp.where(col_odd, left, right), "tile", col_swap)
    side_2 = lax.ppermute(jnp.where(col_odd, right, left), "tile", col_next)

    dspec, resist, terms = pl.pallas_call(
        source_kernel,
        out_shape=(shaped((SPAN, 2 * HALF), BF), shaped((step, TS), BF), shaped((8, 128), F32)),
        in_specs=[SMEM] * 3 + [VMEM] * 5 + [HBM] + [VMEM] * 8,
        out_specs=(VMEM, VMEM, VMEM),
        scratch_shapes=[
            pltpu.VMEM((4, SPAN, 128), F32),
            pltpu.VMEM((groups * own * step, 2 * TS), F32),
            pltpu.VMEM((step, TS), F32),
            pltpu.VMEM((4, SPAN, 128), F32),
            pltpu.VMEM((128, 128), F32),
            pltpu.VMEM((step, TS), jnp.int32),
            pltpu.SemaphoreType.DMA,
        ],
        compiler_params=pltpu.CompilerParams(vmem_limit_bytes=48 << 20),
        name="sources",
    )(
        place, all_shifts, all_weights, mask, vert_1, vert_2, side_1, side_2, target, pupil,
        freq, to_re, to_im, back_t, back, rows, rows_t,
    )

    pieces = [resist] + [src_swap(resist, m, groups) for m in range(1, groups)]
    part = dspec
    for distance in (2, 4, 1):
        other = src_swap(part, distance, groups)
        if distance != 1:
            part = (part.astype(F32) + other.astype(F32)).astype(BF)
    base, rim_1, rim_2, sides = pl.pallas_call(
        mask_kernel,
        out_shape=(
            shaped((TS, TS), F32), shaped((HALO, NE), BF), shaped((HALO, NE), BF), shaped((TS, 2 * HALO), F32),
        ),
        in_specs=[SMEM] + [VMEM] * 6,
        out_specs=(VMEM,) * 4,
        compiler_params=pltpu.CompilerParams(vmem_limit_bytes=40 << 20),
        name="mask_gradient",
    )(place, mask, part, other, to_re, to_im, freq_t)

    got_1 = lax.ppermute(rim_1, "tile", row_swap)
    got_2 = lax.ppermute(rim_2, "tile", row_next)
    send_1, send_2 = pl.pallas_call(
        side_kernel,
        out_shape=(shaped((TS // 2, 128), BF),) * 2,
        in_specs=[SMEM] + [VMEM] * 3,
        out_specs=(VMEM,) * 2,
        scratch_shapes=[pltpu.VMEM((TS, 2 * HALO), F32)],
        name="side_rims",
    )(place, sides, got_1, got_2)
    back_1 = lax.ppermute(send_1, "tile", col_swap)
    back_2 = lax.ppermute(send_2, "tile", col_next)
    new_mask, resist_tile = pl.pallas_call(
        final_kernel,
        out_shape=(shaped((1, TS, TS), F32),) * 2,
        in_specs=[SMEM] + [VMEM] * (5 + groups),
        out_specs=(VMEM,) * 2,
        compiler_params=pltpu.CompilerParams(vmem_limit_bytes=32 << 20),
        name="new_mask",
    )(place, base, got_1, got_2, back_1, back_2, *pieces)

    for distance in (1, 2, 4):
        terms = terms + src_swap(terms, distance, groups)
    for distance in (1, 2, 4, 8, 16):
        terms = terms + tile_swap(terms, distance, tiles)
    weight_total = lax.dynamic_slice(terms, (0, k * own), (1, own))[0]
    new_weights = source_weights - source_rate * weight_total / (TS * TS * tiles)
    return (new_mask, new_weights, resist_tile)


def solution(mesh):
    in_specs = (P("tile", None, None), P("tile", None, None), P("src", None), P("src"), P())
    out_specs = (P("tile", None, None), P("src"), P("tile", None, None))
    return jax.shard_map(
        per_device, mesh=mesh, in_specs=in_specs, out_specs=out_specs, check_vma=False
    )
```

```python
import math

import jax
import jax.numpy as jnp
import ml_dtypes
import numpy as np
from jax import lax
from jax.experimental import pallas as pl
from jax.experimental.pallas import tpu as pltpu
from jax.sharding import PartitionSpec as P

TS = 512
HALO = 64
BAND = 128
SHIFT_MAX = 32
GRID_ROWS = 4
NE = TS + 2 * HALO
SPAN = BAND + 2 * SHIFT_MAX
HALF = 256
FOLD = SPAN // 2
ROWS = FOLD + 16
BATCH = 8
CHUNK = 256

steepness = 10.0
threshold = 0.25
mask_rate = 0.5
source_rate = 8.0

BF = jnp.bfloat16
F32 = jnp.float32

ORDER = np.concatenate([np.arange(HALO, HALO + TS), np.arange(HALO), np.arange(HALO + TS, NE)])


def make_tables():
    freq_index = np.arange(SPAN) - SPAN // 2
    phases = np.mod(freq_index[:, None] * ORDER[None, :], NE) * (2.0 * math.pi / NE)
    freq_re, freq_im = np.cos(phases) / NE, -np.sin(phases) / NE
    band_index = np.arange(BAND) - BAND // 2
    back_phase = np.mod((np.arange(TS) + HALO)[:, None] * band_index[None, :], NE) * (2.0 * math.pi / NE)
    back_re, back_im = np.cos(back_phase), np.sin(back_phase)

    def bf(table):
        return np.ascontiguousarray(table).astype(np.float32).astype(ml_dtypes.bfloat16)

    last = SPAN // 2 * ORDER * (2.0 * math.pi / NE)
    gap = np.zeros((HALF - SPAN - 1, NE))
    freq = np.concatenate([freq_re, np.cos(last)[None] / NE, gap, freq_im, -np.sin(last)[None] / NE, gap], 0)
    kept = np.concatenate([np.arange(FOLD, SPAN), [0]])
    rest = np.zeros((NE, ROWS - FOLD - 1))
    fold_t = np.concatenate([freq_re[kept].T, rest, freq_im[kept].T, rest], 1)
    back_t = np.block([[back_re.T, back_im.T], [-back_im.T, back_re.T]])
    rows = np.concatenate([back_re, back_im], 1)
    return tuple(bf(t) for t in (freq, back_t, back_t.T, rows, fold_t))


def rows_t_table(blocks):
    rows = make_tables()[3]
    step = TS // blocks
    parts = [
        np.concatenate([rows[i * step : (i + 1) * step, :BAND].T, rows[i * step : (i + 1) * step, BAND:].T], 1)
        for i in range(blocks)
    ]
    return np.stack(parts)


def dot(left, right):
    return lax.dot_general(left, right, (((1,), (0,)), ((), ())), preferred_element_type=F32)


def dot_nt(left, right):
    return lax.dot_general(left, right, (((1,), (1,)), ((), ())), preferred_element_type=F32)


def where_am_i():
    columns = lax.axis_size("tile") // GRID_ROWS
    tile = lax.axis_index("tile")
    row = tile // columns
    k = lax.axis_index("src")
    second = k // 2 % 2 == 1
    return k, row % 2 == 1, tile % 2 == 1, (row > 0) & (row < GRID_ROWS - 1), second


def fetch_all(pairs, sems):
    copies = [pltpu.make_async_copy(source, held, sems.at[n]) for n, (source, held) in enumerate(pairs)]
    for copy in copies:
        copy.start()
    return copies


def wait_all(copies):
    for copy in copies:
        copy.wait()


def edge_kernel(
    shifts, weights, mask_at, vert_out, side_1, side_2, info_out, top, bottom, left, right, sems
):
    k, row_odd, col_odd, _inner, second = where_am_i()
    wide = 2 * HALO
    copies = fetch_all(
        (
            (mask_at.at[0, pl.ds(0, HALO), :], top),
            (mask_at.at[0, pl.ds(TS - HALO, HALO), :], bottom),
            (mask_at.at[0, :, pl.ds(0, wide)], left),
            (mask_at.at[0, :, pl.ds(TS - wide, wide)], right),
        ),
        sems,
    )
    own = shifts.shape[1]
    high, low = split(weights[...])
    rest = weights[...] - high.astype(F32)
    mid, low = split(rest)
    parts = [shifts[:1].astype(F32), shifts[1:].astype(F32), high.astype(F32), mid.astype(F32), low.astype(F32)]
    wide_parts = [jnp.concatenate([part, jnp.zeros((1, 128 - own), F32)], 1) for part in parts]
    line = sum(wide_part if n == 0 else pltpu.roll(wide_part, n * own, 1) for n, wide_part in enumerate(wide_parts))
    row = lax.broadcasted_iota(jnp.int32, (16, 128), 0)
    info = jnp.where(row == k, line, 0.0).astype(BF)
    info_out[...] = jnp.concatenate([info, jnp.zeros((16, TS - 128), BF)], 1)
    vert_out[HALO:] = info_out[...]
    wait_all(copies)
    vert_out[:HALO] = jnp.where(row_odd ^ second, top[...], bottom[...]).astype(BF)
    half = TS // 2
    first = lax.broadcasted_iota(jnp.int32, (half, wide), 1) < HALO
    before = jnp.where(first, left[:half], pltpu.roll(left[half:], HALO, 1))
    after = jnp.where(first, pltpu.roll(right[:half], HALO, 1), right[half:])
    side_1[...] = jnp.where(col_odd, before, after).astype(BF)
    side_2[...] = jnp.where(col_odd, after, before).astype(BF)


def corner_kernel(mine_at, theirs_at, side_1_at, side_2_at, send_1, send_2, info_out, held, sems):
    _k, _row_odd, col_odd, _inner, _second = where_am_i()
    wide = 2 * HALO
    half = TS // 2
    ends = (pl.ds(0, wide), pl.ds(TS - wide, wide))
    copies = fetch_all(
        [(got.at[:, end], held.at[2 * n + m]) for n, got in enumerate((mine_at, theirs_at)) for m, end in enumerate(ends)]
        + [(side_1_at, send_1.at[pl.ds(0, half), :]), (side_2_at, send_2.at[pl.ds(0, half), :])],
        sems,
    )
    first = lax.broadcasted_iota(jnp.int32, (HALO, wide), 1) < HALO
    wait_all(copies)

    def above_below(m):
        return arrived(held[m, :HALO], held[2 + m, :HALO])

    info = held[0, HALO:].astype(F32) + held[2, HALO:].astype(F32)
    info_out[...] = info[:8]
    send_1[NE // 2 :] = info.astype(BF)
    above, below = above_below(0)
    before = jnp.where(first, above, pltpu.roll(below, HALO, 1))
    above, below = above_below(1)
    after = jnp.where(first, pltpu.roll(above, HALO, 1), below)
    send_1[half : NE // 2] = jnp.where(col_odd, before, after).astype(BF)
    send_2[half:] = jnp.where(col_odd, after, before).astype(BF)


def source_kernel(
    info, vert_1_at, vert_2_at, side_1_at, side_2_at,
    mask_at, target_at, pupil_at, freq_at, back_t_at, back_at, rows_at, rows_t_at,
    dspec_out, resist_out,
    spec, amps_a, amps_b, fields, image, dspec, terms, vert_1, vert_2, side_1, side_2,
    mask, freq, back_t, back, own_rows, rows_turned, pupil, bits, sems,
):
    step = resist_out.shape[0]
    k, row_odd, col_odd, _inner, second = where_am_i()
    own = pl.ds(pl.multiple_of(k * step, step), step)
    copies = fetch_all(
        (
            (vert_1_at.at[pl.ds(0, HALO), :], vert_1), (vert_2_at.at[pl.ds(0, HALO), :], vert_2),
            (side_1_at.at[pl.ds(0, NE // 2), :], side_1), (side_2_at, side_2),
            (freq_at, freq), (mask_at.at[0], mask), (pupil_at, pupil),
            (rows_at.at[own, :], own_rows), (back_t_at, back_t), (target_at.at[0, own, :], bits),
            (back_at, back), (rows_t_at.at[k], rows_turned),
        ),
        sems,
    )
    image[...] = jnp.zeros_like(image)
    dspec[...] = jnp.zeros_like(dspec)
    terms[...] = jnp.zeros_like(terms)
    wait_all(copies[:6])

    halo_rows = jnp.concatenate(arrived(vert_1[...], vert_2[...]), 0).astype(BF)
    s1, s2 = side_1[...].astype(F32), side_2[...].astype(F32)
    left, right = jnp.where(col_odd, s1, s2), jnp.where(col_odd, s2, s1)
    first = lax.broadcasted_iota(jnp.int32, left.shape, 1) < HALO
    one = jnp.where(first, left, pltpu.roll(right, HALO, 1)).astype(BF)
    two = jnp.where(first, pltpu.roll(left, HALO, 1), right).astype(BF)
    half = TS // 2
    halo_cols = jnp.concatenate([one[:half], two[:half], one[half:], two[half:]], 0)
    prod_mid = dot(freq[:, :TS], mask[...].astype(BF)) + dot(freq[:, TS:], halo_rows)
    prod_side = dot(freq[...], halo_cols)
    prod = jnp.concatenate([prod_mid, prod_side], 1).astype(BF)
    both = dot_nt(prod, freq[...])
    spec_re = both[:SPAN, :HALF] - both[HALF : HALF + SPAN, HALF:]
    spec_im = both[:SPAN, HALF:] + both[HALF : HALF + SPAN, :HALF]
    whole = jnp.concatenate([spec_re, spec_im], 1)
    for j in range(4):
        spec[j] = whole[:, j * 128 : (j + 1) * 128]

    wait_all(copies[6:9])
    gain = pupil[...].astype(F32).astype(BF)
    sources = info.shape[0] * 8

    def where_of(s):
        group, lane = s // 8, s % 8
        down, over = info[group, lane].astype(jnp.int32), info[group, lane + 8].astype(jnp.int32)
        w = (info[group, lane + 16] + info[group, lane + 24]) + info[group, lane + 32]
        return SHIFT_MAX - down, SHIFT_MAX - over, w

    def rows_of(i, u=0, count=BATCH):
        return pl.ds(pl.multiple_of(i * (BATCH * step) + u * step, step), count * step)

    def amplitudes(i, amps):
        for u in range(BATCH):
            down, over, _w = where_of(i * BATCH + u)
            turn = lax.bitwise_and(HALF - over, HALF - 1)
            band = [spec[j, pl.ds(down, BAND), :].astype(BF) for j in range(4)]
            win_re = pltpu.roll(jnp.concatenate(band[:2], 1), turn, 1)[:, :BAND] * gain
            win_im = pltpu.roll(jnp.concatenate(band[2:], 1), turn, 1)[:, :BAND] * gain
            window = jnp.concatenate(
                [jnp.concatenate([win_re, win_im], 1), jnp.concatenate([-win_im, win_re], 1)], 0
            )
            amps[u * step : (u + 1) * step, :] = dot(own_rows[...], window).astype(BF)

    def forward(i, amps):
        for c in range(0, TS, CHUNK):
            field_re = dot(amps[...], back_t[:, c : c + CHUNK])
            field_im = dot(amps[...], back_t[:, TS + c : TS + c + CHUNK])
            fields[rows_of(i), c : c + CHUNK] = field_re
            fields[rows_of(i), TS + c : TS + c + CHUNK] = field_im
            total = image[:, c : c + CHUNK]
            for u in range(BATCH):
                _d, _o, w = where_of(i * BATCH + u)
                re, im = field_re[u * step : (u + 1) * step], field_im[u * step : (u + 1) * step]
                total = total + w * (re * re + im * im)
            image[:, c : c + CHUNK] = total

    batches = sources // BATCH
    amplitudes(0, amps_a)

    def forward_pair(p, _):
        forward(2 * p, amps_a)
        amplitudes(2 * p + 1, amps_b)
        forward(2 * p + 1, amps_b)
        amplitudes(jnp.minimum(2 * p + 2, batches - 1), amps_a)
        return 0

    lax.fori_loop(0, batches // 2, forward_pair, 0)

    wait_all(copies[9:])
    resist = jax.nn.sigmoid(steepness * (image[...] * (1.0 / sources) - threshold))
    resist_out[...] = resist.astype(BF)
    image[...] = 2.0 * (resist - bits[...].astype(F32)) * resist * (1.0 - resist) * steepness

    def backward(i, damps):
        damp = jnp.zeros((BATCH * step, 2 * BAND), F32)
        for c in range(0, TS, CHUNK):
            grad = image[:, c : c + CHUNK]
            parts_re, parts_im = [], []
            for u in range(BATCH):
                s = i * BATCH + u
                _d, _o, w = where_of(s)
                re, im = fields[rows_of(i, u, 1), c : c + CHUNK], fields[rows_of(i, u, 1), TS + c : TS + c + CHUNK]
                term = jnp.sum((grad * (re * re + im * im)).reshape(step // 8, 8, CHUNK), 0)
                terms[s] += sum(term[:, n : n + 128] for n in range(0, CHUNK, 128))
                coef = (2.0 * w / sources) * grad
                parts_re.append((coef * re).astype(BF))
                parts_im.append((coef * im).astype(BF))
            damp = damp + dot(jnp.concatenate(parts_re, 0), back[c : c + CHUNK, :])
            damp = damp + dot(jnp.concatenate(parts_im, 0), back[TS + c : TS + c + CHUNK, :])
        damps[...] = damp.astype(BF)

    empty = jnp.zeros((step, HALF - BAND), BF)
    wide_gain = jnp.concatenate([gain, jnp.zeros((BAND, HALF - BAND), BF)], 1)

    def windows(i, damps):
        for u in range(BATCH):
            down, over, _w = where_of(i * BATCH + u)
            damp = damps[u * step : (u + 1) * step, :]
            damp_re = pltpu.roll(jnp.concatenate([damp[:, :BAND], empty], 1), over, 1)
            damp_im = pltpu.roll(jnp.concatenate([damp[:, BAND:], empty], 1), over, 1)
            inside = pltpu.roll(wide_gain, over, 1).astype(F32)
            pair = jnp.concatenate(
                [jnp.concatenate([damp_re, damp_im], 1), jnp.concatenate([damp_im, -damp_re], 1)], 0
            )
            dwin = dot(rows_turned[...], pair)
            for j in range(4):
                lanes = slice(j % 2 * 128, j % 2 * 128 + 128)
                dspec[u % 2 * 4 + j, pl.ds(down, BAND), :] += dwin[:, j * 128 : (j + 1) * 128] * inside[:, lanes]

    backward(0, amps_a)

    def backward_pair(p, _):
        backward(2 * p + 1, amps_b)
        windows(2 * p, amps_a)
        backward(2 * p + 2, amps_a)
        windows(2 * p + 1, amps_b)
        return 0

    lax.fori_loop(0, batches // 2 - 1, backward_pair, 0)
    backward(batches - 1, amps_b)
    windows(batches - 2, amps_a)
    windows(batches - 1, amps_b)

    whole = jnp.concatenate([dspec[j] + dspec[4 + j] for j in range(4)], 1)
    high, low = split(whole[:FOLD])
    both = jnp.concatenate([high, low], 0)
    turn_cols = (
        lax.broadcasted_iota(jnp.int32, (HALF, HALF), 0) + lax.broadcasted_iota(jnp.int32, (HALF, HALF), 1) == SPAN
    ).astype(BF)
    turned = jnp.concatenate([dot(both[:, :HALF], turn_cols), dot(both[:, HALF:], turn_cols)], 1).astype(BF)
    at_row = lax.broadcasted_iota(jnp.int32, (FOLD, 2 * FOLD), 0)
    at_col = lax.broadcasted_iota(jnp.int32, (FOLD, 2 * FOLD), 1)
    turn_rows = (
        ((at_row + at_col == FOLD) & (at_col < FOLD)) | ((at_row + at_col == 2 * FOLD) & (at_col > FOLD))
    ).astype(BF)
    folded = dot(turn_rows, turned)
    sign = jnp.where(lax.broadcasted_iota(jnp.int32, (FOLD, 2 * HALF), 1) < HALF, 1.0, -1.0)
    dspec_out[:FOLD] = (whole[FOLD:] + sign * folded).astype(BF)
    sums = lax.dot_general(
        jnp.ones((8, 128), F32), jnp.sum(terms[...], 1), (((1,), (1,)), ((), ())),
        precision=lax.Precision.HIGHEST, preferred_element_type=F32,
    )
    dspec_out[FOLD:] = weight_rows(jnp.concatenate([whole[:8], jnp.zeros_like(whole[:8])], 0), sums[:1])


def weight_rows(line, sums):
    high = sums.astype(BF).astype(F32)
    mid = (sums - high).astype(BF).astype(F32)
    low = sums - high - mid
    row = lax.broadcasted_iota(jnp.int32, line.shape, 0)
    kept = jnp.where(row == 0, line, 0.0)
    for n, piece in enumerate((high, mid, low)):
        if line.shape[1] > 128:
            piece = jnp.concatenate([piece, jnp.zeros((1, line.shape[1] - 128), F32)], 1)
        kept = jnp.where(row == n + 1, piece, kept)
    return kept.astype(BF)


def weight_sums(rows):
    return rows[1:2] + rows[2:3] + rows[3:4]


def add(one, two):
    one, two = one.astype(F32), two.astype(F32)
    sums = weight_sums(one[FOLD:]) + weight_sums(two[FOLD:])
    high = lax.reduce_precision(sums, 8, 7)
    mid = lax.reduce_precision(sums - high, 8, 7)
    row = lax.broadcasted_iota(jnp.int32, one.shape, 0) - FOLD
    total = one + two
    for n, piece in enumerate((high, mid, sums - high - mid)):
        total = jnp.where(row == n + 1, piece, total)
    return total.astype(BF)


def split(values):
    high = values.astype(BF)
    return high, (values - high.astype(F32)).astype(BF)


def pack_sides(before, after, col_odd, side_1, side_2):
    side_1[...] = jnp.where(col_odd, before, after).astype(BF)
    side_2[...] = jnp.where(col_odd, after, before).astype(BF)


def mask_kernel(mask, part_1, part_2, freq, fold_t, base_out, rims_out, side_1, side_2):
    _k, _row_odd, col_odd, _inner, _second = where_am_i()
    total = part_1[...].astype(F32) + part_2[...].astype(F32)
    swapped = jnp.concatenate([total[:, HALF:], -total[:, :HALF]], 1)
    both = dot(jnp.concatenate([*split(total), *split(swapped)], 0), freq[...])
    prod = jnp.concatenate([both[:ROWS] + both[ROWS : 2 * ROWS], both[2 * ROWS : 3 * ROWS] + both[3 * ROWS :]], 0)
    high, low = split(prod)
    ext = dot(fold_t[...], high) + dot(fold_t[...], low)
    base_out[...] = mask[0] - mask_rate * ext[:TS, :TS]
    rims_out[...] = ext[TS:, :TS]
    sides = ext[:, TS:]
    half, quarter = TS // 2, HALO
    upper = jnp.concatenate([sides[:half], sides[TS : TS + quarter]], 0)
    lower = jnp.concatenate([sides[half:TS], sides[TS + quarter :]], 0)
    first = lax.broadcasted_iota(jnp.int32, upper.shape, 1) < HALO
    before = jnp.where(first, upper, pltpu.roll(lower, HALO, 1))
    after = jnp.where(first, pltpu.roll(upper, HALO, 1), lower)
    pack_sides(before, after, col_odd, side_1, side_2)


def arrived(mine, theirs):
    mine, theirs = mine.astype(F32), theirs.astype(F32)
    _k, row_odd, _col_odd, inner, second = where_am_i()
    g1 = jnp.where(second, theirs, mine)
    g2 = jnp.where(inner, jnp.where(second, mine, theirs), 0.0)
    return jnp.where(row_odd, g1, g2), jnp.where(row_odd, g2, g1)


def from_sides(side_1, side_2):
    _k, _row_odd, col_odd, _inner, _second = where_am_i()
    s1, s2 = side_1.astype(F32), side_2.astype(F32)
    before, after = jnp.where(col_odd, s1, s2), jnp.where(col_odd, s2, s1)
    first = lax.broadcasted_iota(jnp.int32, before.shape, 1) < HALO
    left = jnp.where(first, before, 0.0), jnp.where(first, pltpu.roll(before, HALO, 1), 0.0)
    right = jnp.where(first, 0.0, pltpu.roll(after, HALO, 1)), jnp.where(first, 0.0, after)
    return left, right


def rim_kernel(rims_at, side_1_at, side_2_at, weight_at, vert_out, rims, side_1, side_2, weight, sems):
    _k, row_odd, _col_odd, _inner, second = where_am_i()
    corner = pl.ds(TS // 2, HALO)
    copies = fetch_all(
        (
            (rims_at, rims), (side_1_at.at[corner, :], side_1), (side_2_at.at[corner, :], side_2), (weight_at, weight),
        ),
        sems,
    )
    wait_all(copies)
    left, right = from_sides(side_1[...], side_2[...])
    wide = 2 * HALO
    for n in range(2):
        rows = slice(n * HALO, (n + 1) * HALO)
        rims[rows, :wide] += left[n]
        rims[rows, TS - wide :] += right[n]
    vert_out[:HALO] = jnp.where(row_odd ^ second, rims[:HALO], rims[HALO:]).astype(BF)
    vert_out[HALO:] = weight_rows(jnp.zeros((16, TS), F32), weight[:1])


def final_kernel(
    base_at, side_1_at, side_2_at, mine_at, theirs_at, weight_at, other_at, near_at, far_at,
    mask_at, resist_at, weight_out,
    base, side_1, side_2, mine, theirs, weight, other, near, far, resist, sems,
):
    k, _row_odd, _col_odd, _inner, second = where_am_i()
    step = near.shape[0] // 4
    half = TS // 2
    inside = (pl.ds(0, half), slice(None))
    copies = fetch_all(
        (
            (near_at, near), (far_at, far), (base_at, base), (side_1_at.at[inside], side_1),
            (side_2_at.at[inside], side_2), (mine_at, mine), (theirs_at, theirs), (weight_at, weight), (other_at, other),
        ),
        sems,
    )
    wait_all(copies[:2])
    for m in range(8):
        piece = (near, far)[m % 2][m // 2 * step : (m // 2 + 1) * step, :]
        at = lax.bitwise_xor(k, m)
        resist[pl.ds(pl.multiple_of(at * step, step), step), :] = piece.astype(F32)
    resist_done = pltpu.make_async_copy(resist, resist_at.at[0], sems.at[0])
    resist_done.start()
    wait_all(copies[2:])
    left, right = from_sides(side_1[...], side_2[...])
    wide = 2 * HALO
    for n in range(2):
        rows = slice(n * half, (n + 1) * half)
        base[rows, :wide] -= mask_rate * left[n]
        base[rows, TS - wide :] -= mask_rate * right[n]
    above, below = arrived(mine[:HALO], theirs[:HALO])
    base[:HALO] -= mask_rate * above
    base[TS - HALO :] -= mask_rate * below
    mask_done = pltpu.make_async_copy(base, mask_at.at[0], sems.at[1])
    mask_done.start()
    from_1, from_2 = weight_sums(mine[HALO:, :128].astype(F32)), weight_sums(theirs[HALO:, :128].astype(F32))
    from_1, from_2 = jnp.where(second, from_2, from_1), jnp.where(second, from_1, from_2)
    weight_out[...] = jnp.broadcast_to((weight[:1] + from_1) + (from_2 + other[:1]), weight_out.shape)
    mask_done.wait()
    resist_done.wait()


SMEM = pl.BlockSpec(memory_space=pltpu.SMEM)
VMEM = pl.BlockSpec(memory_space=pltpu.VMEM)
HBM = pl.BlockSpec(memory_space=pl.ANY)


def shaped(shape, dtype):
    return jax.ShapeDtypeStruct(shape, dtype)


def grid_routes(tiles, columns):
    row_swap = [(t, t ^ columns) for t in range(tiles)]
    row_next = [(t, t + columns) for t in range(tiles) if (t // columns) % 2 == 1 and t + columns < tiles]
    col_swap = [(t, t ^ 1) for t in range(tiles)]
    col_next = [(t, t + 1) for t in range(tiles) if t % 2 == 1 and (t + 1) % columns != 0]
    back = lambda route: route + [(b, a) for a, b in route]
    return row_swap, back(row_next), col_swap, back(col_next)


def route_of(first, second, groups, distance=0):
    return [
        (a * groups + k, b * groups + (k ^ distance)) for k in range(groups) for a, b in (second if k // 2 % 2 == 1 else first)
    ]


def src_swap(block, distance, count):
    return lax.ppermute(block, "src", [(i, i ^ distance) for i in range(count)])


def tile_swap(block, distance, count):
    return lax.ppermute(block, "tile", [(i, i ^ distance) for i in range(count)])


def per_device(mask, target, shifts, source_weights, pupil):
    tiles, groups = lax.axis_size("tile"), lax.axis_size("src")
    columns = tiles // GRID_ROWS
    k = lax.axis_index("src")
    row_swap, row_next, col_swap, col_next = grid_routes(tiles, columns)
    row_ring = row_next + [(t, t ^ (3 * columns)) for t in range(tiles) if (t // columns) % 3 == 0]
    freq, back_t, back, rows, fold_t = (jnp.asarray(t) for t in make_tables())
    rows_t = jnp.asarray(rows_t_table(groups))
    own = shifts.shape[0]
    step = TS // groups

    vert, side_1, side_2, info = pl.pallas_call(
        edge_kernel,
        out_shape=(shaped((HALO + 16, TS), BF),) + (shaped((TS // 2, 128), BF),) * 2 + (shaped((16, TS), BF),),
        in_specs=[VMEM] * 2 + [HBM],
        out_specs=(VMEM,) * 4,
        scratch_shapes=[pltpu.VMEM((HALO, TS), F32)] * 2
        + [pltpu.VMEM((TS, 2 * HALO), F32)] * 2
        + [pltpu.SemaphoreType.DMA((4,))],
        name="edges",
    )(shifts.T, source_weights[None], mask)
    mine = lax.ppermute(vert, ("tile", "src"), route_of(row_swap, row_ring, groups, 4))
    mine = jnp.concatenate([mine[:HALO], mine[HALO:] + info], 0)
    theirs = src_swap(mine, 2, groups)
    side_1, side_2, info = pl.pallas_call(
        corner_kernel,
        out_shape=(shaped((NE // 2 + 16, 128), BF), shaped((NE // 2, 128), BF), shaped((8, 128), F32)),
        in_specs=[HBM] * 4,
        out_specs=(VMEM,) * 3,
        scratch_shapes=[pltpu.VMEM((4, HALO + 16, 2 * HALO), BF), pltpu.SemaphoreType.DMA((6,))],
        name="corners",
    )(mine, theirs, side_1, side_2)
    side_1 = lax.ppermute(side_1, ("tile", "src"), route_of(col_swap, col_swap, groups, 1))
    side_2 = lax.ppermute(side_2, "tile", col_next)
    info = info + side_1[NE // 2 : NE // 2 + 8].astype(F32)

    part, resist = pl.pallas_call(
        source_kernel,
        out_shape=(shaped((ROWS, 2 * HALF), BF), shaped((step, TS), BF)),
        in_specs=[SMEM] + [HBM] * 12,
        out_specs=(VMEM, VMEM),
        scratch_shapes=[
            pltpu.VMEM((4, SPAN, 128), F32),
            pltpu.VMEM((BATCH * step, 2 * BAND), BF),
            pltpu.VMEM((BATCH * step, 2 * BAND), BF),
            pltpu.VMEM((groups * own * step, 2 * TS), F32),
            pltpu.VMEM((step, TS), F32),
            pltpu.VMEM((8, SPAN, 128), F32),
            pltpu.VMEM((128, 8, 128), F32),
            pltpu.VMEM((HALO, TS), BF),
            pltpu.VMEM((HALO, TS), BF),
            pltpu.VMEM((NE // 2, 128), BF),
            pltpu.VMEM((NE // 2, 128), BF),
            pltpu.VMEM((TS, TS), F32),
            pltpu.VMEM((2 * HALF, NE), BF),
            pltpu.VMEM((2 * BAND, 2 * TS), BF),
            pltpu.VMEM((2 * TS, 2 * BAND), BF),
            pltpu.VMEM((step, 2 * BAND), BF),
            pltpu.VMEM((BAND, 2 * step), BF),
            pltpu.VMEM((BAND, BAND), jnp.int32),
            pltpu.VMEM((step, TS), jnp.int32),
            pltpu.SemaphoreType.DMA((12,)),
        ],
        compiler_params=pltpu.CompilerParams(vmem_limit_bytes=60 << 20),
        name="sources",
    )(
        info, mine, theirs, side_1, side_2, mask, target, pupil,
        freq, back_t, back, rows, rows_t,
    )

    other = src_swap(part, 2, groups)
    near = src_swap(resist, 2, groups)
    part, near = lax.optimization_barrier((add(part, other), near))
    other = src_swap(part, 4, groups)
    part = add(part, other)
    other = src_swap(part, 1, groups)
    weight = weight_sums(part[FOLD:, :128].astype(F32)) + weight_sums(other[FOLD:, :128].astype(F32))
    weight = jnp.broadcast_to(weight, (8, 128))
    weight = weight + tile_swap(weight, 1, tiles)
    base, rims, side_1, side_2 = pl.pallas_call(
        mask_kernel,
        out_shape=(shaped((TS, TS), F32), shaped((2 * HALO, TS), F32)) + (shaped((NE // 2, 128), BF),) * 2,
        in_specs=[VMEM] * 5,
        out_specs=(VMEM,) * 4,
        compiler_params=pltpu.CompilerParams(vmem_limit_bytes=40 << 20),
        name="mask_gradient",
    )(mask, part, other, freq, fold_t)

    near = jnp.concatenate([resist, near], 0)
    side_1, side_2, weight, near = lax.optimization_barrier((side_1, side_2, weight, near))
    far = src_swap(near, 4, groups)
    side_1 = lax.ppermute(side_1, "tile", col_swap)
    side_2 = lax.ppermute(side_2, "tile", col_next)
    for distance in (2, 4):
        weight = weight + tile_swap(weight, distance, tiles)
    side_1, side_2, weight, far = lax.optimization_barrier((side_1, side_2, weight, far))
    rim = pl.pallas_call(
        rim_kernel,
        out_shape=shaped((HALO + 16, TS), BF),
        in_specs=[HBM] * 4,
        out_specs=VMEM,
        scratch_shapes=[
            pltpu.VMEM((2 * HALO, TS), F32),
            pltpu.VMEM((HALO, 128), BF),
            pltpu.VMEM((HALO, 128), BF),
            pltpu.VMEM((8, 128), F32),
            pltpu.SemaphoreType.DMA((4,)),
        ],
        name="row_rims",
    )(rims, side_1, side_2, weight)
    near = jnp.concatenate([near, far], 0)
    rim, weight, near = lax.optimization_barrier((rim, weight, near))
    mine = lax.ppermute(rim, ("tile", "src"), route_of(row_swap, row_ring, groups))
    other = tile_swap(weight, 2 * columns, tiles)
    far = src_swap(near, 1, groups)
    theirs = src_swap(mine, 2, groups)
    new_mask, resist_tile, terms = pl.pallas_call(
        final_kernel,
        out_shape=(shaped((1, TS, TS), F32),) * 2 + (shaped((8, 128), F32),),
        in_specs=[HBM] * 9,
        out_specs=(HBM, HBM, VMEM),
        scratch_shapes=[
            pltpu.VMEM((TS, TS), F32),
            pltpu.VMEM((TS // 2, 128), BF),
            pltpu.VMEM((TS // 2, 128), BF),
            pltpu.VMEM((HALO + 16, TS), BF),
            pltpu.VMEM((HALO + 16, TS), BF),
            pltpu.VMEM((8, 128), F32),
            pltpu.VMEM((8, 128), F32),
            pltpu.VMEM((4 * step, TS), BF),
            pltpu.VMEM((4 * step, TS), BF),
            pltpu.VMEM((TS, TS), F32),
            pltpu.SemaphoreType.DMA((9,)),
        ],
        name="new_mask",
    )(base, side_1, side_2, mine, theirs, weight, other, near, far)

    weight_total = lax.dynamic_slice(terms, (0, k * own), (1, own))[0]
    new_weights = source_weights - source_rate * weight_total / (TS * TS * tiles)
    return (new_mask, new_weights, resist_tile)


def solution(mesh):
    in_specs = (P("tile", None, None), P("tile", None, None), P("src", None), P("src"), P())
    out_specs = (P("tile", None, None), P("src"), P("tile", None, None))
    return jax.shard_map(
        per_device, mesh=mesh, in_specs=in_specs, out_specs=out_specs, check_vma=False
    )
```

```python
import math

import jax
import jax.numpy as jnp
import ml_dtypes
import numpy as np
from jax import lax
from jax.experimental import pallas as pl
from jax.experimental.pallas import tpu as pltpu
from jax.sharding import PartitionSpec as P

TS = 512
HALO = 64
BAND = 128
SHIFT_MAX = 32
GRID_ROWS = 4
NE = TS + 2 * HALO
SPAN = BAND + 2 * SHIFT_MAX
HALF = 256
FOLD = SPAN // 2
ROWS = FOLD + 16
BATCH = 8
CHUNK = 256

steepness = 10.0
threshold = 0.25
mask_rate = 0.5
source_rate = 8.0

BF = jnp.bfloat16
F32 = jnp.float32

ORDER = np.concatenate([np.arange(HALO, HALO + TS), np.arange(HALO), np.arange(HALO + TS, NE)])


def make_tables():
    freq_index = np.arange(SPAN) - SPAN // 2
    phases = np.mod(freq_index[:, None] * ORDER[None, :], NE) * (2.0 * math.pi / NE)
    freq_re, freq_im = np.cos(phases) / NE, -np.sin(phases) / NE
    band_index = np.arange(BAND) - BAND // 2
    back_phase = np.mod((np.arange(TS) + HALO)[:, None] * band_index[None, :], NE) * (2.0 * math.pi / NE)
    back_re, back_im = np.cos(back_phase), np.sin(back_phase)

    def bf(table):
        return np.ascontiguousarray(table).astype(np.float32).astype(ml_dtypes.bfloat16)

    last = SPAN // 2 * ORDER * (2.0 * math.pi / NE)
    gap = np.zeros((HALF - SPAN - 1, NE))
    freq = np.concatenate([freq_re, np.cos(last)[None] / NE, gap, freq_im, -np.sin(last)[None] / NE, gap], 0)
    kept = np.concatenate([np.arange(FOLD, SPAN), [0]])
    rest = np.zeros((NE, ROWS - FOLD - 1))
    fold_t = np.concatenate([freq_re[kept].T, rest, freq_im[kept].T, rest], 1)
    back_t = np.block([[back_re.T, back_im.T], [-back_im.T, back_re.T]])
    rows = np.concatenate([back_re, back_im], 1)
    return tuple(bf(t) for t in (freq, back_t, back_t.T, rows, fold_t))


def rows_t_table(blocks):
    rows = make_tables()[3]
    step = TS // blocks
    parts = [
        np.concatenate([rows[i * step : (i + 1) * step, :BAND].T, rows[i * step : (i + 1) * step, BAND:].T], 1)
        for i in range(blocks)
    ]
    return np.stack(parts)


def dot(left, right):
    return lax.dot_general(left, right, (((1,), (0,)), ((), ())), preferred_element_type=F32)


def dot_nt(left, right):
    return lax.dot_general(left, right, (((1,), (1,)), ((), ())), preferred_element_type=F32)


def where_am_i():
    columns = lax.axis_size("tile") // GRID_ROWS
    tile = lax.axis_index("tile")
    row = tile // columns
    k = lax.axis_index("src")
    second = k // 2 % 2 == 1
    return k, row % 2 == 1, tile % 2 == 1, (row > 0) & (row < GRID_ROWS - 1), second


def fetch_all(pairs, sems):
    copies = [pltpu.make_async_copy(source, held, sems.at[n]) for n, (source, held) in enumerate(pairs)]
    for copy in copies:
        copy.start()
    return copies


def wait_all(copies):
    for copy in copies:
        copy.wait()


def edge_kernel(
    shifts, weights, mask_at, vert_out, side_1, side_2, info_out, top, bottom, left, right, sems
):
    k, row_odd, col_odd, _inner, second = where_am_i()
    wide = 2 * HALO
    copies = fetch_all(
        (
            (mask_at.at[0, pl.ds(0, HALO), :], top),
            (mask_at.at[0, pl.ds(TS - HALO, HALO), :], bottom),
            (mask_at.at[0, :, pl.ds(0, wide)], left),
            (mask_at.at[0, :, pl.ds(TS - wide, wide)], right),
        ),
        sems,
    )
    own = shifts.shape[1]
    high, low = split(weights[...])
    rest = weights[...] - high.astype(F32)
    mid, low = split(rest)
    parts = [shifts[:1].astype(F32), shifts[1:].astype(F32), high.astype(F32), mid.astype(F32), low.astype(F32)]
    wide_parts = [jnp.concatenate([part, jnp.zeros((1, 128 - own), F32)], 1) for part in parts]
    line = sum(wide_part if n == 0 else pltpu.roll(wide_part, n * own, 1) for n, wide_part in enumerate(wide_parts))
    row = lax.broadcasted_iota(jnp.int32, (16, 128), 0)
    info = jnp.where(row == k, line, 0.0).astype(BF)
    info_out[...] = jnp.concatenate([info, jnp.zeros((16, TS - 128), BF)], 1)
    vert_out[HALO:] = info_out[...]
    wait_all(copies)
    vert_out[:HALO] = jnp.where(row_odd ^ second, top[...], bottom[...]).astype(BF)
    half = TS // 2
    first = lax.broadcasted_iota(jnp.int32, (half, wide), 1) < HALO
    before = jnp.where(first, left[:half], pltpu.roll(left[half:], HALO, 1))
    after = jnp.where(first, pltpu.roll(right[:half], HALO, 1), right[half:])
    side_1[...] = jnp.where(col_odd, before, after).astype(BF)
    side_2[...] = jnp.where(col_odd, after, before).astype(BF)


def corner_kernel(mine, theirs, side_1, side_2, send_1, send_2, info_out):
    _k, _row_odd, col_odd, _inner, _second = where_am_i()
    wide = 2 * HALO
    half = TS // 2
    ends = (slice(0, wide), slice(TS - wide, TS))
    send_1[:half] = side_1[...]
    send_2[:half] = side_2[...]
    first = lax.broadcasted_iota(jnp.int32, (HALO, wide), 1) < HALO

    def above_below(m):
        return arrived(mine[:HALO, ends[m]], theirs[:HALO, ends[m]])

    info = mine[HALO:, :wide].astype(F32) + theirs[HALO:, :wide].astype(F32)
    info_out[...] = info[:8]
    send_1[NE // 2 :] = info.astype(BF)
    above, below = above_below(0)
    before = jnp.where(first, above, pltpu.roll(below, HALO, 1))
    above, below = above_below(1)
    after = jnp.where(first, pltpu.roll(above, HALO, 1), below)
    send_1[half : NE // 2] = jnp.where(col_odd, before, after).astype(BF)
    send_2[half:] = jnp.where(col_odd, after, before).astype(BF)


def source_kernel(
    info, mine, theirs, side_1, side_2,
    mask_at, target_at, pupil_at, freq_at, back_t_at, back_at, rows_at, rows_t_at,
    dspec_out, resist_out,
    spec, amps_a, amps_b, fields, image, dspec, terms,
    mask, freq, back_t, back, own_rows, rows_turned, pupil, bits, sems,
):
    step = resist_out.shape[0]
    k, row_odd, col_odd, _inner, second = where_am_i()
    own = pl.ds(pl.multiple_of(k * step, step), step)
    copies = fetch_all(
        (
            (freq_at, freq), (mask_at.at[0], mask), (pupil_at, pupil),
            (rows_at.at[own, :], own_rows), (back_t_at, back_t), (target_at.at[0, own, :], bits),
            (back_at, back), (rows_t_at.at[k], rows_turned),
        ),
        sems,
    )
    image[...] = jnp.zeros_like(image)
    dspec[...] = jnp.zeros_like(dspec)
    terms[...] = jnp.zeros_like(terms)
    wait_all(copies[:2])

    halo_rows = jnp.concatenate(arrived(mine[:HALO], theirs[:HALO]), 0).astype(BF)
    s1, s2 = side_1[: NE // 2].astype(F32), side_2[...].astype(F32)
    left, right = jnp.where(col_odd, s1, s2), jnp.where(col_odd, s2, s1)
    first = lax.broadcasted_iota(jnp.int32, left.shape, 1) < HALO
    one = jnp.where(first, left, pltpu.roll(right, HALO, 1)).astype(BF)
    two = jnp.where(first, pltpu.roll(left, HALO, 1), right).astype(BF)
    half = TS // 2
    halo_cols = jnp.concatenate([one[:half], two[:half], one[half:], two[half:]], 0)
    prod_mid = dot(freq[:, :TS], mask[...].astype(BF)) + dot(freq[:, TS:], halo_rows)
    prod_side = dot(freq[...], halo_cols)
    prod = jnp.concatenate([prod_mid, prod_side], 1).astype(BF)
    both = dot_nt(prod, freq[...])
    spec_re = both[:SPAN, :HALF] - both[HALF : HALF + SPAN, HALF:]
    spec_im = both[:SPAN, HALF:] + both[HALF : HALF + SPAN, :HALF]
    whole = jnp.concatenate([spec_re, spec_im], 1)
    for j in range(4):
        spec[j] = whole[:, j * 128 : (j + 1) * 128]

    wait_all(copies[2:5])
    gain = pupil[...].astype(F32).astype(BF)
    sources = info.shape[0] * 8

    def where_of(s):
        group, lane = s // 8, s % 8
        down, over = info[group, lane].astype(jnp.int32), info[group, lane + 8].astype(jnp.int32)
        w = (info[group, lane + 16] + info[group, lane + 24]) + info[group, lane + 32]
        return SHIFT_MAX - down, SHIFT_MAX - over, w

    def rows_of(i, u=0, count=BATCH):
        return pl.ds(pl.multiple_of(i * (BATCH * step) + u * step, step), count * step)

    def amplitudes(i, amps):
        for u in range(BATCH):
            down, over, _w = where_of(i * BATCH + u)
            turn = lax.bitwise_and(HALF - over, HALF - 1)
            band = [spec[j, pl.ds(down, BAND), :].astype(BF) for j in range(4)]
            win_re = pltpu.roll(jnp.concatenate(band[:2], 1), turn, 1)[:, :BAND] * gain
            win_im = pltpu.roll(jnp.concatenate(band[2:], 1), turn, 1)[:, :BAND] * gain
            window = jnp.concatenate(
                [jnp.concatenate([win_re, win_im], 1), jnp.concatenate([-win_im, win_re], 1)], 0
            )
            amps[u * step : (u + 1) * step, :] = dot(own_rows[...], window).astype(BF)

    def forward(i, amps):
        for c in range(0, TS, CHUNK):
            field_re = dot(amps[...], back_t[:, c : c + CHUNK])
            field_im = dot(amps[...], back_t[:, TS + c : TS + c + CHUNK])
            fields[rows_of(i), c : c + CHUNK] = field_re
            fields[rows_of(i), TS + c : TS + c + CHUNK] = field_im
            total = image[:, c : c + CHUNK]
            for u in range(BATCH):
                _d, _o, w = where_of(i * BATCH + u)
                re, im = field_re[u * step : (u + 1) * step], field_im[u * step : (u + 1) * step]
                total = total + w * (re * re + im * im)
            image[:, c : c + CHUNK] = total

    batches = sources // BATCH
    amplitudes(0, amps_a)

    def forward_pair(p, _):
        forward(2 * p, amps_a)
        amplitudes(2 * p + 1, amps_b)
        forward(2 * p + 1, amps_b)
        amplitudes(jnp.minimum(2 * p + 2, batches - 1), amps_a)
        return 0

    lax.fori_loop(0, batches // 2, forward_pair, 0)

    wait_all(copies[5:])
    resist = jax.nn.sigmoid(steepness * (image[...] * (1.0 / sources) - threshold))
    resist_out[...] = resist.astype(BF)
    image[...] = 2.0 * (resist - bits[...].astype(F32)) * resist * (1.0 - resist) * steepness

    def backward(i, damps):
        damp = jnp.zeros((BATCH * step, 2 * BAND), F32)
        for c in range(0, TS, CHUNK):
            grad = image[:, c : c + CHUNK]
            parts_re, parts_im = [], []
            for u in range(BATCH):
                s = i * BATCH + u
                _d, _o, w = where_of(s)
                re, im = fields[rows_of(i, u, 1), c : c + CHUNK], fields[rows_of(i, u, 1), TS + c : TS + c + CHUNK]
                term = jnp.sum((grad * (re * re + im * im)).reshape(step // 8, 8, CHUNK), 0)
                terms[s] += sum(term[:, n : n + 128] for n in range(0, CHUNK, 128))
                coef = (2.0 * w / sources) * grad
                parts_re.append((coef * re).astype(BF))
                parts_im.append((coef * im).astype(BF))
            damp = damp + dot(jnp.concatenate(parts_re, 0), back[c : c + CHUNK, :])
            damp = damp + dot(jnp.concatenate(parts_im, 0), back[TS + c : TS + c + CHUNK, :])
        damps[...] = damp.astype(BF)

    empty = jnp.zeros((step, HALF - BAND), BF)
    wide_gain = jnp.concatenate([gain, jnp.zeros((BAND, HALF - BAND), BF)], 1)

    def windows(i, damps):
        for u in range(BATCH):
            down, over, _w = where_of(i * BATCH + u)
            damp = damps[u * step : (u + 1) * step, :]
            damp_re = pltpu.roll(jnp.concatenate([damp[:, :BAND], empty], 1), over, 1)
            damp_im = pltpu.roll(jnp.concatenate([damp[:, BAND:], empty], 1), over, 1)
            inside = pltpu.roll(wide_gain, over, 1).astype(F32)
            pair = jnp.concatenate(
                [jnp.concatenate([damp_re, damp_im], 1), jnp.concatenate([damp_im, -damp_re], 1)], 0
            )
            dwin = dot(rows_turned[...], pair)
            for j in range(4):
                lanes = slice(j % 2 * 128, j % 2 * 128 + 128)
                dspec[u % 2 * 4 + j, pl.ds(down, BAND), :] += dwin[:, j * 128 : (j + 1) * 128] * inside[:, lanes]

    backward(0, amps_a)

    def backward_pair(p, _):
        backward(2 * p + 1, amps_b)
        windows(2 * p, amps_a)
        backward(2 * p + 2, amps_a)
        windows(2 * p + 1, amps_b)
        return 0

    lax.fori_loop(0, batches // 2 - 1, backward_pair, 0)
    backward(batches - 1, amps_b)
    windows(batches - 2, amps_a)
    windows(batches - 1, amps_b)

    whole = jnp.concatenate([dspec[j] + dspec[4 + j] for j in range(4)], 1)
    high, low = split(whole[:FOLD])
    both = jnp.concatenate([high, low], 0)
    turn_cols = (
        lax.broadcasted_iota(jnp.int32, (HALF, HALF), 0) + lax.broadcasted_iota(jnp.int32, (HALF, HALF), 1) == SPAN
    ).astype(BF)
    turned = jnp.concatenate([dot(both[:, :HALF], turn_cols), dot(both[:, HALF:], turn_cols)], 1).astype(BF)
    at_row = lax.broadcasted_iota(jnp.int32, (FOLD, 2 * FOLD), 0)
    at_col = lax.broadcasted_iota(jnp.int32, (FOLD, 2 * FOLD), 1)
    turn_rows = (
        ((at_row + at_col == FOLD) & (at_col < FOLD)) | ((at_row + at_col == 2 * FOLD) & (at_col > FOLD))
    ).astype(BF)
    folded = dot(turn_rows, turned)
    sign = jnp.where(lax.broadcasted_iota(jnp.int32, (FOLD, 2 * HALF), 1) < HALF, 1.0, -1.0)
    dspec_out[:FOLD] = (whole[FOLD:] + sign * folded).astype(BF)
    sums = lax.dot_general(
        jnp.ones((8, 128), F32), jnp.sum(terms[...], 1), (((1,), (1,)), ((), ())),
        precision=lax.Precision.HIGHEST, preferred_element_type=F32,
    )
    dspec_out[FOLD:] = weight_rows(jnp.concatenate([whole[:8], jnp.zeros_like(whole[:8])], 0), sums[:1])


def weight_rows(line, sums):
    high = sums.astype(BF).astype(F32)
    mid = (sums - high).astype(BF).astype(F32)
    low = sums - high - mid
    row = lax.broadcasted_iota(jnp.int32, line.shape, 0)
    kept = jnp.where(row == 0, line, 0.0)
    for n, piece in enumerate((high, mid, low)):
        if line.shape[1] > 128:
            piece = jnp.concatenate([piece, jnp.zeros((1, line.shape[1] - 128), F32)], 1)
        kept = jnp.where(row == n + 1, piece, kept)
    return kept.astype(BF)


def weight_sums(rows):
    return rows[1:2] + rows[2:3] + rows[3:4]


def add(one, two):
    one, two = one.astype(F32), two.astype(F32)
    sums = weight_sums(one[FOLD:]) + weight_sums(two[FOLD:])
    high = lax.reduce_precision(sums, 8, 7)
    mid = lax.reduce_precision(sums - high, 8, 7)
    row = lax.broadcasted_iota(jnp.int32, one.shape, 0) - FOLD
    total = one + two
    for n, piece in enumerate((high, mid, sums - high - mid)):
        total = jnp.where(row == n + 1, piece, total)
    return total.astype(BF)


def split(values):
    high = values.astype(BF)
    return high, (values - high.astype(F32)).astype(BF)


def pack_sides(before, after, col_odd, side_1, side_2):
    side_1[...] = jnp.where(col_odd, before, after).astype(BF)
    side_2[...] = jnp.where(col_odd, after, before).astype(BF)


def mask_kernel(mask, part_1, part_2, freq, fold_t, base_out, rims_out, side_1, side_2):
    _k, _row_odd, col_odd, _inner, _second = where_am_i()
    total = part_1[...].astype(F32) + part_2[...].astype(F32)
    swapped = jnp.concatenate([total[:, HALF:], -total[:, :HALF]], 1)
    both = dot(jnp.concatenate([*split(total), *split(swapped)], 0), freq[...])
    prod = jnp.concatenate([both[:ROWS] + both[ROWS : 2 * ROWS], both[2 * ROWS : 3 * ROWS] + both[3 * ROWS :]], 0)
    high, low = split(prod)
    ext = dot(fold_t[...], high) + dot(fold_t[...], low)
    base_out[...] = mask[0] - mask_rate * ext[:TS, :TS]
    rims_out[...] = ext[TS:, :TS]
    sides = ext[:, TS:]
    half, quarter = TS // 2, HALO
    upper = jnp.concatenate([sides[:half], sides[TS : TS + quarter]], 0)
    lower = jnp.concatenate([sides[half:TS], sides[TS + quarter :]], 0)
    first = lax.broadcasted_iota(jnp.int32, upper.shape, 1) < HALO
    before = jnp.where(first, upper, pltpu.roll(lower, HALO, 1))
    after = jnp.where(first, pltpu.roll(upper, HALO, 1), lower)
    pack_sides(before, after, col_odd, side_1, side_2)


def arrived(mine, theirs):
    mine, theirs = mine.astype(F32), theirs.astype(F32)
    _k, row_odd, _col_odd, inner, second = where_am_i()
    g1 = jnp.where(second, theirs, mine)
    g2 = jnp.where(inner, jnp.where(second, mine, theirs), 0.0)
    return jnp.where(row_odd, g1, g2), jnp.where(row_odd, g2, g1)


def from_sides(side_1, side_2):
    _k, _row_odd, col_odd, _inner, _second = where_am_i()
    s1, s2 = side_1.astype(F32), side_2.astype(F32)
    before, after = jnp.where(col_odd, s1, s2), jnp.where(col_odd, s2, s1)
    first = lax.broadcasted_iota(jnp.int32, before.shape, 1) < HALO
    left = jnp.where(first, before, 0.0), jnp.where(first, pltpu.roll(before, HALO, 1), 0.0)
    right = jnp.where(first, 0.0, pltpu.roll(after, HALO, 1)), jnp.where(first, 0.0, after)
    return left, right


def rim_kernel(rims_in, side_1, side_2, weight, vert_out, rims):
    _k, row_odd, _col_odd, _inner, second = where_am_i()
    rims[...] = rims_in[...]
    left, right = from_sides(side_1[TS // 2 :], side_2[TS // 2 :])
    wide = 2 * HALO
    for n in range(2):
        rows = slice(n * HALO, (n + 1) * HALO)
        rims[rows, :wide] += left[n]
        rims[rows, TS - wide :] += right[n]
    vert_out[:HALO] = jnp.where(row_odd ^ second, rims[:HALO], rims[HALO:]).astype(BF)
    vert_out[HALO:] = weight_rows(jnp.zeros((16, TS), F32), weight[:1])


def final_kernel(
    base_in, side_1, side_2, mine, theirs, weight, other, near, far, source_weights,
    mask_at, resist_at, weights_out, base, resist, sems,
):
    k, _row_odd, _col_odd, _inner, second = where_am_i()
    step = near.shape[0] // 4
    half = TS // 2
    for m in range(8):
        piece = (near, far)[m % 2][m // 2 * step : (m // 2 + 1) * step, :]
        at = lax.bitwise_xor(k, m)
        resist[pl.ds(pl.multiple_of(at * step, step), step), :] = piece.astype(F32)
    resist_done = pltpu.make_async_copy(resist, resist_at.at[0], sems.at[0])
    resist_done.start()
    base[...] = base_in[...]
    left, right = from_sides(side_1[:half], side_2[:half])
    wide = 2 * HALO
    for n in range(2):
        rows = slice(n * half, (n + 1) * half)
        base[rows, :wide] -= mask_rate * left[n]
        base[rows, TS - wide :] -= mask_rate * right[n]
    above, below = arrived(mine[:HALO], theirs[:HALO])
    base[:HALO] -= mask_rate * above
    base[TS - HALO :] -= mask_rate * below
    mask_done = pltpu.make_async_copy(base, mask_at.at[0], sems.at[1])
    mask_done.start()
    from_1, from_2 = weight_sums(mine[HALO:, :128].astype(F32)), weight_sums(theirs[HALO:, :128].astype(F32))
    from_1, from_2 = jnp.where(second, from_2, from_1), jnp.where(second, from_1, from_2)
    total = (weight[:1] + from_1) + (from_2 + other[:1])
    own = source_weights.shape[1]
    total = pltpu.roll(jnp.broadcast_to(total, (8, 128)), lax.bitwise_and(128 - own * k, 127), 1)
    tiles = lax.axis_size("tile")
    weights_out[...] = source_weights[...] - source_rate * total[:1, :own] / (TS * TS * tiles)
    mask_done.wait()
    resist_done.wait()


SMEM = pl.BlockSpec(memory_space=pltpu.SMEM)
VMEM = pl.BlockSpec(memory_space=pltpu.VMEM)
HBM = pl.BlockSpec(memory_space=pl.ANY)


def shaped(shape, dtype):
    return jax.ShapeDtypeStruct(shape, dtype)


def grid_routes(tiles, columns):
    row_swap = [(t, t ^ columns) for t in range(tiles)]
    row_next = [(t, t + columns) for t in range(tiles) if (t // columns) % 2 == 1 and t + columns < tiles]
    col_swap = [(t, t ^ 1) for t in range(tiles)]
    col_next = [(t, t + 1) for t in range(tiles) if t % 2 == 1 and (t + 1) % columns != 0]
    back = lambda route: route + [(b, a) for a, b in route]
    return row_swap, back(row_next), col_swap, back(col_next)


def route_of(first, second, groups, distance=0):
    return [
        (a * groups + k, b * groups + (k ^ distance)) for k in range(groups) for a, b in (second if k // 2 % 2 == 1 else first)
    ]


def src_swap(block, distance, count):
    return lax.ppermute(block, "src", [(i, i ^ distance) for i in range(count)])


def tile_swap(block, distance, count):
    return lax.ppermute(block, "tile", [(i, i ^ distance) for i in range(count)])


def per_device(mask, target, shifts, source_weights, pupil):
    tiles, groups = lax.axis_size("tile"), lax.axis_size("src")
    columns = tiles // GRID_ROWS
    k = lax.axis_index("src")
    row_swap, row_next, col_swap, col_next = grid_routes(tiles, columns)
    row_ring = row_next + [(t, t ^ (3 * columns)) for t in range(tiles) if (t // columns) % 3 == 0]
    freq, back_t, back, rows, fold_t = (jnp.asarray(t) for t in make_tables())
    rows_t = jnp.asarray(rows_t_table(groups))
    own = shifts.shape[0]
    step = TS // groups

    vert, side_1, side_2, info = pl.pallas_call(
        edge_kernel,
        out_shape=(shaped((HALO + 16, TS), BF),) + (shaped((TS // 2, 128), BF),) * 2 + (shaped((16, TS), BF),),
        in_specs=[VMEM] * 2 + [HBM],
        out_specs=(VMEM,) * 4,
        scratch_shapes=[pltpu.VMEM((HALO, TS), F32)] * 2
        + [pltpu.VMEM((TS, 2 * HALO), F32)] * 2
        + [pltpu.SemaphoreType.DMA((4,))],
        name="edges",
    )(shifts.T, source_weights[None], mask)
    mine = lax.ppermute(vert, ("tile", "src"), route_of(row_swap, row_ring, groups, 4))
    mine = jnp.concatenate([mine[:HALO], mine[HALO:] + info], 0)
    theirs = src_swap(mine, 2, groups)
    side_1, side_2, info = pl.pallas_call(
        corner_kernel,
        out_shape=(shaped((NE // 2 + 16, 128), BF), shaped((NE // 2, 128), BF), shaped((8, 128), F32)),
        in_specs=[VMEM] * 4,
        out_specs=(VMEM,) * 3,
        name="corners",
    )(mine, theirs, side_1, side_2)
    side_1 = lax.ppermute(side_1, ("tile", "src"), route_of(col_swap, col_swap, groups, 1))
    side_2 = lax.ppermute(side_2, "tile", col_next)
    info = info + side_1[NE // 2 : NE // 2 + 8].astype(F32)

    part, resist = pl.pallas_call(
        source_kernel,
        out_shape=(shaped((ROWS, 2 * HALF), BF), shaped((step, TS), BF)),
        in_specs=[SMEM] + [VMEM] * 4 + [HBM] * 8,
        out_specs=(VMEM, VMEM),
        scratch_shapes=[
            pltpu.VMEM((4, SPAN, 128), F32),
            pltpu.VMEM((BATCH * step, 2 * BAND), BF),
            pltpu.VMEM((BATCH * step, 2 * BAND), BF),
            pltpu.VMEM((groups * own * step, 2 * TS), F32),
            pltpu.VMEM((step, TS), F32),
            pltpu.VMEM((8, SPAN, 128), F32),
            pltpu.VMEM((128, 8, 128), F32),
            pltpu.VMEM((TS, TS), F32),
            pltpu.VMEM((2 * HALF, NE), BF),
            pltpu.VMEM((2 * BAND, 2 * TS), BF),
            pltpu.VMEM((2 * TS, 2 * BAND), BF),
            pltpu.VMEM((step, 2 * BAND), BF),
            pltpu.VMEM((BAND, 2 * step), BF),
            pltpu.VMEM((BAND, BAND), jnp.int32),
            pltpu.VMEM((step, TS), jnp.int32),
            pltpu.SemaphoreType.DMA((8,)),
        ],
        compiler_params=pltpu.CompilerParams(vmem_limit_bytes=60 << 20),
        name="sources",
    )(
        info, mine, theirs, side_1, side_2, mask, target, pupil,
        freq, back_t, back, rows, rows_t,
    )

    other = src_swap(part, 2, groups)
    near = src_swap(resist, 2, groups)
    part = add(part, other)
    other = src_swap(part, 4, groups)
    part, near = lax.optimization_barrier((add(part, other), near))
    other = src_swap(part, 1, groups)
    weight = weight_sums(part[FOLD:, :128].astype(F32)) + weight_sums(other[FOLD:, :128].astype(F32))
    weight = jnp.broadcast_to(weight, (8, 128))
    weight = weight + tile_swap(weight, 1, tiles)
    base, rims, side_1, side_2 = pl.pallas_call(
        mask_kernel,
        out_shape=(shaped((TS, TS), F32), shaped((2 * HALO, TS), F32)) + (shaped((NE // 2, 128), BF),) * 2,
        in_specs=[VMEM] * 5,
        out_specs=(VMEM,) * 4,
        compiler_params=pltpu.CompilerParams(vmem_limit_bytes=40 << 20),
        name="mask_gradient",
    )(mask, part, other, freq, fold_t)

    near = jnp.concatenate([resist, near], 0)
    side_1, side_2, weight, near = lax.optimization_barrier((side_1, side_2, weight, near))
    far = src_swap(near, 4, groups)
    side_1 = lax.ppermute(side_1, "tile", col_swap)
    side_2 = lax.ppermute(side_2, "tile", col_next)
    for distance in (2, 4):
        weight = weight + tile_swap(weight, distance, tiles)
    side_1, side_2, weight, far = lax.optimization_barrier((side_1, side_2, weight, far))
    rim = pl.pallas_call(
        rim_kernel,
        out_shape=shaped((HALO + 16, TS), BF),
        in_specs=[VMEM] * 4,
        out_specs=VMEM,
        scratch_shapes=[pltpu.VMEM((2 * HALO, TS), F32)],
        name="row_rims",
    )(rims, side_1, side_2, weight)
    near = jnp.concatenate([near, far], 0)
    rim, weight, near = lax.optimization_barrier((rim, weight, near))
    mine = lax.ppermute(rim, ("tile", "src"), route_of(row_swap, row_ring, groups))
    other = tile_swap(weight, 2 * columns, tiles)
    far = src_swap(near, 1, groups)
    theirs = src_swap(mine, 2, groups)
    new_mask, resist_tile, new_weights = pl.pallas_call(
        final_kernel,
        out_shape=(shaped((1, TS, TS), F32),) * 2 + (shaped((1, own), F32),),
        in_specs=[VMEM] * 10,
        out_specs=(HBM, HBM, VMEM),
        scratch_shapes=[
            pltpu.VMEM((TS, TS), F32),
            pltpu.VMEM((TS, TS), F32),
            pltpu.SemaphoreType.DMA((2,)),
        ],
        compiler_params=pltpu.CompilerParams(vmem_limit_bytes=24 << 20),
        name="new_mask",
    )(base, side_1, side_2, mine, theirs, weight, other, near, far, source_weights[None])

    return (new_mask, new_weights[0], resist_tile)


def solution(mesh):
    in_specs = (P("tile", None, None), P("tile", None, None), P("src", None), P("src"), P())
    out_specs = (P("tile", None, None), P("src"), P("tile", None, None))
    return jax.shard_map(
        per_device, mesh=mesh, in_specs=in_specs, out_specs=out_specs, check_vma=False
    )
```

```python
import math

import jax
import jax.numpy as jnp
import ml_dtypes
import numpy as np
from jax import lax
from jax.experimental import pallas as pl
from jax.experimental.pallas import tpu as pltpu
from jax.sharding import PartitionSpec as P

TS = 512
HALO = 64
BAND = 128
SHIFT_MAX = 32
GRID_ROWS = 4
NE = TS + 2 * HALO
SPAN = BAND + 2 * SHIFT_MAX
HALF = 256
FOLD = SPAN // 2
ROWS = FOLD + 16
BATCH = 8
CHUNK = 256

steepness = 10.0
threshold = 0.25
mask_rate = 0.5
source_rate = 8.0

BF = jnp.bfloat16
F32 = jnp.float32

ORDER = np.concatenate([np.arange(HALO, HALO + TS), np.arange(HALO), np.arange(HALO + TS, NE)])


def make_tables():
    freq_index = np.arange(SPAN) - SPAN // 2
    phases = np.mod(freq_index[:, None] * ORDER[None, :], NE) * (2.0 * math.pi / NE)
    freq_re, freq_im = np.cos(phases) / NE, -np.sin(phases) / NE
    band_index = np.arange(BAND) - BAND // 2
    back_phase = np.mod((np.arange(TS) + HALO)[:, None] * band_index[None, :], NE) * (2.0 * math.pi / NE)
    back_re, back_im = np.cos(back_phase), np.sin(back_phase)

    def bf(table):
        return np.ascontiguousarray(table).astype(np.float32).astype(ml_dtypes.bfloat16)

    last = SPAN // 2 * ORDER * (2.0 * math.pi / NE)
    gap = np.zeros((HALF - SPAN - 1, NE))
    freq = np.concatenate([freq_re, np.cos(last)[None] / NE, gap, freq_im, -np.sin(last)[None] / NE, gap], 0)
    kept = np.concatenate([np.arange(FOLD, SPAN), [0]])
    rest = np.zeros((NE, ROWS - FOLD - 1))
    fold_t = np.concatenate([freq_re[kept].T, rest, freq_im[kept].T, rest], 1)
    back_t = np.block([[back_re.T, back_im.T], [-back_im.T, back_re.T]])
    rows = np.concatenate([back_re, back_im], 1)
    return tuple(bf(t) for t in (freq, back_t, back_t.T, rows, fold_t))


def rows_t_table(blocks):
    rows = make_tables()[3]
    step = TS // blocks
    parts = [
        np.concatenate([rows[i * step : (i + 1) * step, :BAND].T, rows[i * step : (i + 1) * step, BAND:].T], 1)
        for i in range(blocks)
    ]
    return np.stack(parts)


def dot(left, right):
    return lax.dot_general(left, right, (((1,), (0,)), ((), ())), preferred_element_type=F32)


def dot_nt(left, right):
    return lax.dot_general(left, right, (((1,), (1,)), ((), ())), preferred_element_type=F32)


def where_am_i():
    columns = lax.axis_size("tile") // GRID_ROWS
    tile = lax.axis_index("tile")
    row = tile // columns
    k = lax.axis_index("src")
    second = k // 2 % 2 == 1
    return k, row % 2 == 1, tile % 2 == 1, (row > 0) & (row < GRID_ROWS - 1), second


def fetch_all(pairs, sems):
    copies = [pltpu.make_async_copy(source, held, sems.at[n]) for n, (source, held) in enumerate(pairs)]
    for copy in copies:
        copy.start()
    return copies


def wait_all(copies):
    for copy in copies:
        copy.wait()


def edge_kernel(
    shifts, weights, mask_at, vert_out, side_1, side_2, info_out, top, bottom, left, right, sems
):
    k, row_odd, col_odd, _inner, second = where_am_i()
    wide = 2 * HALO
    copies = fetch_all(
        (
            (mask_at.at[0, pl.ds(0, HALO), :], top),
            (mask_at.at[0, pl.ds(TS - HALO, HALO), :], bottom),
            (mask_at.at[0, :, pl.ds(0, wide)], left),
            (mask_at.at[0, :, pl.ds(TS - wide, wide)], right),
        ),
        sems,
    )
    own = shifts.shape[1]
    high, low = split(weights[...])
    rest = weights[...] - high.astype(F32)
    mid, low = split(rest)
    parts = [shifts[:1].astype(F32), shifts[1:].astype(F32), high.astype(F32), mid.astype(F32), low.astype(F32)]
    wide_parts = [jnp.concatenate([part, jnp.zeros((1, 128 - own), F32)], 1) for part in parts]
    line = sum(wide_part if n == 0 else pltpu.roll(wide_part, n * own, 1) for n, wide_part in enumerate(wide_parts))
    row = lax.broadcasted_iota(jnp.int32, (16, 128), 0)
    info = jnp.where(row == k, line, 0.0).astype(BF)
    info_out[...] = jnp.concatenate([info, jnp.zeros((16, TS - 128), BF)], 1)
    vert_out[HALO:] = info_out[...]
    wait_all(copies)
    vert_out[:HALO] = jnp.where(row_odd ^ second, top[...], bottom[...]).astype(BF)
    half = TS // 2
    first = lax.broadcasted_iota(jnp.int32, (half, wide), 1) < HALO
    before = jnp.where(first, left[:half], pltpu.roll(left[half:], HALO, 1))
    after = jnp.where(first, pltpu.roll(right[:half], HALO, 1), right[half:])
    side_1[...] = jnp.where(col_odd, before, after).astype(BF)
    side_2[...] = jnp.where(col_odd, after, before).astype(BF)


def corner_kernel(mine, theirs, side_1, side_2, send_1, send_2, info_out):
    _k, _row_odd, col_odd, _inner, _second = where_am_i()
    wide = 2 * HALO
    half = TS // 2
    ends = (slice(0, wide), slice(TS - wide, TS))
    send_1[:half] = side_1[...]
    send_2[:half] = side_2[...]
    first = lax.broadcasted_iota(jnp.int32, (HALO, wide), 1) < HALO

    def above_below(m):
        return arrived(mine[:HALO, ends[m]], theirs[:HALO, ends[m]])

    info = mine[HALO:, :wide].astype(F32) + theirs[HALO:, :wide].astype(F32)
    info_out[...] = info[:8]
    send_1[NE // 2 :] = info.astype(BF)
    above, below = above_below(0)
    before = jnp.where(first, above, pltpu.roll(below, HALO, 1))
    above, below = above_below(1)
    after = jnp.where(first, pltpu.roll(above, HALO, 1), below)
    send_1[half : NE // 2] = jnp.where(col_odd, before, after).astype(BF)
    send_2[half:] = jnp.where(col_odd, after, before).astype(BF)


def source_kernel(
    info, mine, theirs, side_1, side_2,
    mask_at, target_at, pupil_at, freq_at, back_t_at, back_at, rows_at, rows_t_at,
    dspec_out, resist_out,
    spec, amps_a, amps_b, fields, image, dspec, terms,
    mask, freq, back_t, back, own_rows, rows_turned, pupil, bits, sems,
):
    step = resist_out.shape[0]
    k, row_odd, col_odd, _inner, second = where_am_i()
    own = pl.ds(pl.multiple_of(k * step, step), step)
    copies = fetch_all(
        (
            (freq_at, freq), (mask_at.at[0], mask), (pupil_at, pupil),
            (rows_at.at[own, :], own_rows), (back_t_at, back_t), (target_at.at[0, own, :], bits),
            (back_at, back), (rows_t_at.at[k], rows_turned),
        ),
        sems,
    )
    image[...] = jnp.zeros_like(image)
    dspec[...] = jnp.zeros_like(dspec)
    terms[...] = jnp.zeros_like(terms)
    wait_all(copies[:2])

    halo_rows = jnp.concatenate(arrived(mine[:HALO], theirs[:HALO]), 0).astype(BF)
    s1, s2 = side_1[: NE // 2].astype(F32), side_2[...].astype(F32)
    left, right = jnp.where(col_odd, s1, s2), jnp.where(col_odd, s2, s1)
    first = lax.broadcasted_iota(jnp.int32, left.shape, 1) < HALO
    one = jnp.where(first, left, pltpu.roll(right, HALO, 1)).astype(BF)
    two = jnp.where(first, pltpu.roll(left, HALO, 1), right).astype(BF)
    half = TS // 2
    halo_cols = jnp.concatenate([one[:half], two[:half], one[half:], two[half:]], 0)
    prod_mid = dot(freq[:, :TS], mask[...].astype(BF)) + dot(freq[:, TS:], halo_rows)
    prod_side = dot(freq[...], halo_cols)
    prod = jnp.concatenate([prod_mid, prod_side], 1).astype(BF)
    both = dot_nt(prod, freq[...])
    spec_re = both[:SPAN, :HALF] - both[HALF : HALF + SPAN, HALF:]
    spec_im = both[:SPAN, HALF:] + both[HALF : HALF + SPAN, :HALF]
    whole = jnp.concatenate([spec_re, spec_im], 1)
    for j in range(4):
        spec[j] = whole[:, j * 128 : (j + 1) * 128]

    wait_all(copies[2:5])
    gain = pupil[...].astype(F32).astype(BF)
    sources = info.shape[0] * 8

    def where_of(s):
        group, lane = s // 8, s % 8
        down, over = info[group, lane].astype(jnp.int32), info[group, lane + 8].astype(jnp.int32)
        w = (info[group, lane + 16] + info[group, lane + 24]) + info[group, lane + 32]
        return SHIFT_MAX - down, SHIFT_MAX - over, w

    def rows_of(i, u=0, count=BATCH):
        return pl.ds(pl.multiple_of(i * (BATCH * step) + u * step, step), count * step)

    def amplitudes(i, amps):
        for u in range(BATCH):
            down, over, _w = where_of(i * BATCH + u)
            turn = lax.bitwise_and(HALF - over, HALF - 1)
            band = [spec[j, pl.ds(down, BAND), :].astype(BF) for j in range(4)]
            win_re = pltpu.roll(jnp.concatenate(band[:2], 1), turn, 1)[:, :BAND] * gain
            win_im = pltpu.roll(jnp.concatenate(band[2:], 1), turn, 1)[:, :BAND] * gain
            window = jnp.concatenate(
                [jnp.concatenate([win_re, win_im], 1), jnp.concatenate([-win_im, win_re], 1)], 0
            )
            amps[u * step : (u + 1) * step, :] = dot(own_rows[...], window).astype(BF)

    def forward(i, amps):
        for c in range(0, TS, CHUNK):
            field_re = dot(amps[...], back_t[:, c : c + CHUNK])
            field_im = dot(amps[...], back_t[:, TS + c : TS + c + CHUNK])
            fields[rows_of(i), c : c + CHUNK] = field_re
            fields[rows_of(i), TS + c : TS + c + CHUNK] = field_im
            total = image[:, c : c + CHUNK]
            for u in range(BATCH):
                _d, _o, w = where_of(i * BATCH + u)
                re, im = field_re[u * step : (u + 1) * step], field_im[u * step : (u + 1) * step]
                total = total + w * (re * re + im * im)
            image[:, c : c + CHUNK] = total

    batches = sources // BATCH
    amplitudes(0, amps_a)

    def forward_pair(p, _):
        forward(2 * p, amps_a)
        amplitudes(2 * p + 1, amps_b)
        forward(2 * p + 1, amps_b)
        amplitudes(jnp.minimum(2 * p + 2, batches - 1), amps_a)
        return 0

    lax.fori_loop(0, batches // 2, forward_pair, 0)

    wait_all(copies[5:])
    resist = jax.nn.sigmoid(steepness * (image[...] * (1.0 / sources) - threshold))
    resist_out[...] = resist.astype(BF)
    image[...] = 2.0 * (resist - bits[...].astype(F32)) * resist * (1.0 - resist) * steepness

    def backward(i, damps):
        damp = jnp.zeros((BATCH * step, 2 * BAND), F32)
        for c in range(0, TS, CHUNK):
            grad = image[:, c : c + CHUNK]
            parts_re, parts_im = [], []
            for u in range(BATCH):
                s = i * BATCH + u
                _d, _o, w = where_of(s)
                re, im = fields[rows_of(i, u, 1), c : c + CHUNK], fields[rows_of(i, u, 1), TS + c : TS + c + CHUNK]
                term = jnp.sum((grad * (re * re + im * im)).reshape(step // 8, 8, CHUNK), 0)
                terms[s] += sum(term[:, n : n + 128] for n in range(0, CHUNK, 128))
                coef = (2.0 * w / sources) * grad
                parts_re.append((coef * re).astype(BF))
                parts_im.append((coef * im).astype(BF))
            damp = damp + dot(jnp.concatenate(parts_re, 0), back[c : c + CHUNK, :])
            damp = damp + dot(jnp.concatenate(parts_im, 0), back[TS + c : TS + c + CHUNK, :])
        damps[...] = damp.astype(BF)

    empty = jnp.zeros((step, HALF - BAND), BF)
    wide_gain = jnp.concatenate([gain, jnp.zeros((BAND, HALF - BAND), BF)], 1)

    def windows(i, damps):
        for u in range(BATCH):
            down, over, _w = where_of(i * BATCH + u)
            damp = damps[u * step : (u + 1) * step, :]
            damp_re = pltpu.roll(jnp.concatenate([damp[:, :BAND], empty], 1), over, 1)
            damp_im = pltpu.roll(jnp.concatenate([damp[:, BAND:], empty], 1), over, 1)
            inside = pltpu.roll(wide_gain, over, 1).astype(F32)
            pair = jnp.concatenate(
                [jnp.concatenate([damp_re, damp_im], 1), jnp.concatenate([damp_im, -damp_re], 1)], 0
            )
            dwin = dot(rows_turned[...], pair)
            for j in range(4):
                lanes = slice(j % 2 * 128, j % 2 * 128 + 128)
                dspec[u % 2 * 4 + j, pl.ds(down, BAND), :] += dwin[:, j * 128 : (j + 1) * 128] * inside[:, lanes]

    backward(0, amps_a)

    def backward_pair(p, _):
        backward(2 * p + 1, amps_b)
        windows(2 * p, amps_a)
        backward(2 * p + 2, amps_a)
        windows(2 * p + 1, amps_b)
        return 0

    lax.fori_loop(0, batches // 2 - 1, backward_pair, 0)
    backward(batches - 1, amps_b)
    windows(batches - 2, amps_a)
    windows(batches - 1, amps_b)

    whole = jnp.concatenate([dspec[j] + dspec[4 + j] for j in range(4)], 1)
    high, low = split(whole[:FOLD])
    both = jnp.concatenate([high, low], 0)
    turn_cols = (
        lax.broadcasted_iota(jnp.int32, (HALF, HALF), 0) + lax.broadcasted_iota(jnp.int32, (HALF, HALF), 1) == SPAN
    ).astype(BF)
    turned = jnp.concatenate([dot(both[:, :HALF], turn_cols), dot(both[:, HALF:], turn_cols)], 1).astype(BF)
    at_row = lax.broadcasted_iota(jnp.int32, (FOLD, 2 * FOLD), 0)
    at_col = lax.broadcasted_iota(jnp.int32, (FOLD, 2 * FOLD), 1)
    turn_rows = (
        ((at_row + at_col == FOLD) & (at_col < FOLD)) | ((at_row + at_col == 2 * FOLD) & (at_col > FOLD))
    ).astype(BF)
    folded = dot(turn_rows, turned)
    sign = jnp.where(lax.broadcasted_iota(jnp.int32, (FOLD, 2 * HALF), 1) < HALF, 1.0, -1.0)
    dspec_out[:FOLD] = (whole[FOLD:] + sign * folded).astype(BF)
    sums = lax.dot_general(
        jnp.ones((8, 128), F32), jnp.sum(terms[...], 1), (((1,), (1,)), ((), ())),
        precision=lax.Precision.HIGHEST, preferred_element_type=F32,
    )
    dspec_out[FOLD:] = weight_rows(jnp.concatenate([whole[:8], jnp.zeros_like(whole[:8])], 0), sums[:1])


def weight_rows(line, sums):
    high = sums.astype(BF).astype(F32)
    mid = (sums - high).astype(BF).astype(F32)
    low = sums - high - mid
    row = lax.broadcasted_iota(jnp.int32, line.shape, 0)
    kept = jnp.where(row == 0, line, 0.0)
    for n, piece in enumerate((high, mid, low)):
        if line.shape[1] > 128:
            piece = jnp.concatenate([piece, jnp.zeros((1, line.shape[1] - 128), F32)], 1)
        kept = jnp.where(row == n + 1, piece, kept)
    return kept.astype(BF)


def weight_sums(rows):
    return rows[1:2] + rows[2:3] + rows[3:4]


def add(*parts):
    parts = [part.astype(F32) for part in parts]
    rows = [weight_sums(part[FOLD:]) for part in parts]
    sums = (rows[0] + rows[1]) + (rows[2] + rows[3])
    total = (parts[0] + parts[1]) + (parts[2] + parts[3])
    high = lax.reduce_precision(sums, 8, 7)
    mid = lax.reduce_precision(sums - high, 8, 7)
    row = lax.broadcasted_iota(jnp.int32, total.shape, 0) - FOLD
    for n, piece in enumerate((high, mid, sums - high - mid)):
        total = jnp.where(row == n + 1, piece, total)
    return total.astype(BF)


def split(values):
    high = values.astype(BF)
    return high, (values - high.astype(F32)).astype(BF)


def pack_sides(before, after, col_odd, side_1, side_2):
    side_1[...] = jnp.where(col_odd, before, after).astype(BF)
    side_2[...] = jnp.where(col_odd, after, before).astype(BF)


def mask_kernel(mask, part_1, part_2, freq, fold_t, base_out, rims_out, side_1, side_2):
    _k, _row_odd, col_odd, _inner, _second = where_am_i()
    total = part_1[...].astype(F32) + part_2[...].astype(F32)
    swapped = jnp.concatenate([total[:, HALF:], -total[:, :HALF]], 1)
    both = dot(jnp.concatenate([*split(total), *split(swapped)], 0), freq[...])
    prod = jnp.concatenate([both[:ROWS] + both[ROWS : 2 * ROWS], both[2 * ROWS : 3 * ROWS] + both[3 * ROWS :]], 0)
    high, low = split(prod)
    ext = dot(fold_t[...], high) + dot(fold_t[...], low)
    base_out[...] = mask[0] - mask_rate * ext[:TS, :TS]
    rims_out[...] = ext[TS:, :TS]
    sides = ext[:, TS:]
    half, quarter = TS // 2, HALO
    upper = jnp.concatenate([sides[:half], sides[TS : TS + quarter]], 0)
    lower = jnp.concatenate([sides[half:TS], sides[TS + quarter :]], 0)
    first = lax.broadcasted_iota(jnp.int32, upper.shape, 1) < HALO
    before = jnp.where(first, upper, pltpu.roll(lower, HALO, 1))
    after = jnp.where(first, pltpu.roll(upper, HALO, 1), lower)
    pack_sides(before, after, col_odd, side_1, side_2)


def arrived(mine, theirs):
    mine, theirs = mine.astype(F32), theirs.astype(F32)
    _k, row_odd, _col_odd, inner, second = where_am_i()
    g1 = jnp.where(second, theirs, mine)
    g2 = jnp.where(inner, jnp.where(second, mine, theirs), 0.0)
    return jnp.where(row_odd, g1, g2), jnp.where(row_odd, g2, g1)


def from_sides(side_1, side_2):
    _k, _row_odd, col_odd, _inner, _second = where_am_i()
    s1, s2 = side_1.astype(F32), side_2.astype(F32)
    before, after = jnp.where(col_odd, s1, s2), jnp.where(col_odd, s2, s1)
    first = lax.broadcasted_iota(jnp.int32, before.shape, 1) < HALO
    left = jnp.where(first, before, 0.0), jnp.where(first, pltpu.roll(before, HALO, 1), 0.0)
    right = jnp.where(first, 0.0, pltpu.roll(after, HALO, 1)), jnp.where(first, 0.0, after)
    return left, right


def rim_kernel(rims_in, side_1, side_2, weight, vert_out, rims):
    _k, row_odd, _col_odd, _inner, second = where_am_i()
    rims[...] = rims_in[...]
    left, right = from_sides(side_1[TS // 2 :], side_2[TS // 2 :])
    wide = 2 * HALO
    for n in range(2):
        rows = slice(n * HALO, (n + 1) * HALO)
        rims[rows, :wide] += left[n]
        rims[rows, TS - wide :] += right[n]
    vert_out[:HALO] = jnp.where(row_odd ^ second, rims[:HALO], rims[HALO:]).astype(BF)
    vert_out[HALO:] = weight_rows(jnp.zeros((16, TS), F32), weight[:1])


def final_kernel(
    base_in, side_1, side_2, mine, theirs, weight, other, near, far, source_weights,
    mask_at, resist_at, weights_out, base, resist, sems,
):
    k, _row_odd, _col_odd, _inner, second = where_am_i()
    step = near.shape[0] // 4
    half = TS // 2
    for m in range(8):
        piece = (near, far)[m % 2][m // 2 * step : (m // 2 + 1) * step, :]
        at = lax.bitwise_xor(k, m)
        resist[pl.ds(pl.multiple_of(at * step, step), step), :] = piece.astype(F32)
    resist_done = pltpu.make_async_copy(resist, resist_at.at[0], sems.at[0])
    resist_done.start()
    base[...] = base_in[...]
    left, right = from_sides(side_1[:half], side_2[:half])
    wide = 2 * HALO
    for n in range(2):
        rows = slice(n * half, (n + 1) * half)
        base[rows, :wide] -= mask_rate * left[n]
        base[rows, TS - wide :] -= mask_rate * right[n]
    above, below = arrived(mine[:HALO], theirs[:HALO])
    base[:HALO] -= mask_rate * above
    base[TS - HALO :] -= mask_rate * below
    mask_done = pltpu.make_async_copy(base, mask_at.at[0], sems.at[1])
    mask_done.start()
    from_1, from_2 = weight_sums(mine[HALO:, :128].astype(F32)), weight_sums(theirs[HALO:, :128].astype(F32))
    from_1, from_2 = jnp.where(second, from_2, from_1), jnp.where(second, from_1, from_2)
    total = (weight[:1] + from_1) + (from_2 + other[:1])
    own = source_weights.shape[1]
    total = pltpu.roll(jnp.broadcast_to(total, (8, 128)), lax.bitwise_and(128 - own * k, 127), 1)
    tiles = lax.axis_size("tile")
    weights_out[...] = source_weights[...] - source_rate * total[:1, :own] / (TS * TS * tiles)
    mask_done.wait()
    resist_done.wait()


SMEM = pl.BlockSpec(memory_space=pltpu.SMEM)
VMEM = pl.BlockSpec(memory_space=pltpu.VMEM)
HBM = pl.BlockSpec(memory_space=pl.ANY)


def shaped(shape, dtype):
    return jax.ShapeDtypeStruct(shape, dtype)


def grid_routes(tiles, columns):
    row_swap = [(t, t ^ columns) for t in range(tiles)]
    row_next = [(t, t + columns) for t in range(tiles) if (t // columns) % 2 == 1 and t + columns < tiles]
    col_swap = [(t, t ^ 1) for t in range(tiles)]
    col_next = [(t, t + 1) for t in range(tiles) if t % 2 == 1 and (t + 1) % columns != 0]
    back = lambda route: route + [(b, a) for a, b in route]
    return row_swap, back(row_next), col_swap, back(col_next)


def route_of(first, second, groups, distance=0):
    return [
        (a * groups + k, b * groups + (k ^ distance)) for k in range(groups) for a, b in (second if k // 2 % 2 == 1 else first)
    ]


def src_swap(block, distance, count):
    return lax.ppermute(block, "src", [(i, i ^ distance) for i in range(count)])


def tile_swap(block, distance, count):
    return lax.ppermute(block, "tile", [(i, i ^ distance) for i in range(count)])


def per_device(mask, target, shifts, source_weights, pupil):
    tiles, groups = lax.axis_size("tile"), lax.axis_size("src")
    columns = tiles // GRID_ROWS
    k = lax.axis_index("src")
    row_swap, row_next, col_swap, col_next = grid_routes(tiles, columns)
    row_ring = row_next + [(t, t ^ (3 * columns)) for t in range(tiles) if (t // columns) % 3 == 0]
    freq, back_t, back, rows, fold_t = (jnp.asarray(t) for t in make_tables())
    rows_t = jnp.asarray(rows_t_table(groups))
    own = shifts.shape[0]
    step = TS // groups

    vert, side_1, side_2, info = pl.pallas_call(
        edge_kernel,
        out_shape=(shaped((HALO + 16, TS), BF),) + (shaped((TS // 2, 128), BF),) * 2 + (shaped((16, TS), BF),),
        in_specs=[VMEM] * 2 + [HBM],
        out_specs=(VMEM,) * 4,
        scratch_shapes=[pltpu.VMEM((HALO, TS), F32)] * 2
        + [pltpu.VMEM((TS, 2 * HALO), F32)] * 2
        + [pltpu.SemaphoreType.DMA((4,))],
        name="edges",
    )(shifts.T, source_weights[None], mask)
    mine = lax.ppermute(vert, ("tile", "src"), route_of(row_swap, row_ring, groups, 4))
    mine = jnp.concatenate([mine[:HALO], mine[HALO:] + info], 0)
    theirs = src_swap(mine, 2, groups)
    side_1, side_2, info = pl.pallas_call(
        corner_kernel,
        out_shape=(shaped((NE // 2 + 16, 128), BF), shaped((NE // 2, 128), BF), shaped((8, 128), F32)),
        in_specs=[VMEM] * 4,
        out_specs=(VMEM,) * 3,
        name="corners",
    )(mine, theirs, side_1, side_2)
    side_1 = lax.ppermute(side_1, ("tile", "src"), route_of(col_swap, col_swap, groups, 1))
    side_2 = lax.ppermute(side_2, "tile", col_next)
    info = info + side_1[NE // 2 : NE // 2 + 8].astype(F32)

    part, resist = pl.pallas_call(
        source_kernel,
        out_shape=(shaped((ROWS, 2 * HALF), BF), shaped((step, TS), BF)),
        in_specs=[SMEM] + [VMEM] * 4 + [HBM] * 8,
        out_specs=(VMEM, VMEM),
        scratch_shapes=[
            pltpu.VMEM((4, SPAN, 128), F32),
            pltpu.VMEM((BATCH * step, 2 * BAND), BF),
            pltpu.VMEM((BATCH * step, 2 * BAND), BF),
            pltpu.VMEM((groups * own * step, 2 * TS), F32),
            pltpu.VMEM((step, TS), F32),
            pltpu.VMEM((8, SPAN, 128), F32),
            pltpu.VMEM((128, 8, 128), F32),
            pltpu.VMEM((TS, TS), F32),
            pltpu.VMEM((2 * HALF, NE), BF),
            pltpu.VMEM((2 * BAND, 2 * TS), BF),
            pltpu.VMEM((2 * TS, 2 * BAND), BF),
            pltpu.VMEM((step, 2 * BAND), BF),
            pltpu.VMEM((BAND, 2 * step), BF),
            pltpu.VMEM((BAND, BAND), jnp.int32),
            pltpu.VMEM((step, TS), jnp.int32),
            pltpu.SemaphoreType.DMA((8,)),
        ],
        compiler_params=pltpu.CompilerParams(vmem_limit_bytes=60 << 20),
        name="sources",
    )(
        info, mine, theirs, side_1, side_2, mask, target, pupil,
        freq, back_t, back, rows, rows_t,
    )

    near = src_swap(resist, 2, groups)
    part = add(part, *(src_swap(part, distance, groups) for distance in (2, 4, 6)))
    other = src_swap(part, 1, groups)
    weight = weight_sums(part[FOLD:, :128].astype(F32)) + weight_sums(other[FOLD:, :128].astype(F32))
    weight = jnp.broadcast_to(weight, (8, 128))
    weight = weight + tile_swap(weight, 1, tiles)
    base, rims, side_1, side_2 = pl.pallas_call(
        mask_kernel,
        out_shape=(shaped((TS, TS), F32), shaped((2 * HALO, TS), F32)) + (shaped((NE // 2, 128), BF),) * 2,
        in_specs=[VMEM] * 5,
        out_specs=(VMEM,) * 4,
        compiler_params=pltpu.CompilerParams(vmem_limit_bytes=40 << 20),
        name="mask_gradient",
    )(mask, part, other, freq, fold_t)

    near = jnp.concatenate([resist, near], 0)
    side_1, side_2, weight, near = lax.optimization_barrier((side_1, side_2, weight, near))
    far = src_swap(near, 4, groups)
    side_1 = lax.ppermute(side_1, "tile", col_swap)
    side_2 = lax.ppermute(side_2, "tile", col_next)
    for distance in (2, 4):
        weight = weight + tile_swap(weight, distance, tiles)
    side_1, side_2, weight, far = lax.optimization_barrier((side_1, side_2, weight, far))
    rim = pl.pallas_call(
        rim_kernel,
        out_shape=shaped((HALO + 16, TS), BF),
        in_specs=[VMEM] * 4,
        out_specs=VMEM,
        scratch_shapes=[pltpu.VMEM((2 * HALO, TS), F32)],
        name="row_rims",
    )(rims, side_1, side_2, weight)
    near = jnp.concatenate([near, far], 0)
    rim, weight, near = lax.optimization_barrier((rim, weight, near))
    mine = lax.ppermute(rim, ("tile", "src"), route_of(row_swap, row_ring, groups))
    other = tile_swap(weight, 2 * columns, tiles)
    far = src_swap(near, 1, groups)
    theirs = src_swap(mine, 2, groups)
    new_mask, resist_tile, new_weights = pl.pallas_call(
        final_kernel,
        out_shape=(shaped((1, TS, TS), F32),) * 2 + (shaped((1, own), F32),),
        in_specs=[VMEM] * 10,
        out_specs=(HBM, HBM, VMEM),
        scratch_shapes=[
            pltpu.VMEM((TS, TS), F32),
            pltpu.VMEM((TS, TS), F32),
            pltpu.SemaphoreType.DMA((2,)),
        ],
        compiler_params=pltpu.CompilerParams(vmem_limit_bytes=24 << 20),
        name="new_mask",
    )(base, side_1, side_2, mine, theirs, weight, other, near, far, source_weights[None])

    return (new_mask, new_weights[0], resist_tile)


def solution(mesh):
    in_specs = (P("tile", None, None), P("tile", None, None), P("src", None), P("src"), P())
    out_specs = (P("tile", None, None), P("src"), P("tile", None, None))
    return jax.shard_map(
        per_device, mesh=mesh, in_specs=in_specs, out_specs=out_specs, check_vma=False
    )
```

```python
import math

import jax
import jax.numpy as jnp
import ml_dtypes
import numpy as np
from jax import lax
from jax.experimental import pallas as pl
from jax.experimental.pallas import tpu as pltpu
from jax.sharding import PartitionSpec as P

TS = 512
HALO = 64
BAND = 128
SHIFT_MAX = 32
GRID_ROWS = 4
NE = TS + 2 * HALO
SPAN = BAND + 2 * SHIFT_MAX
HALF = 256
FOLD = SPAN // 2
ROWS = FOLD + 16
BATCH = 8
CHUNK = 256

steepness = 10.0
threshold = 0.25
mask_rate = 0.5
source_rate = 8.0

BF = jnp.bfloat16
F32 = jnp.float32

ORDER = np.concatenate([np.arange(HALO, HALO + TS), np.arange(HALO), np.arange(HALO + TS, NE)])


def make_tables():
    freq_index = np.arange(SPAN) - SPAN // 2
    phases = np.mod(freq_index[:, None] * ORDER[None, :], NE) * (2.0 * math.pi / NE)
    freq_re, freq_im = np.cos(phases) / NE, -np.sin(phases) / NE
    band_index = np.arange(BAND) - BAND // 2
    back_phase = np.mod((np.arange(TS) + HALO)[:, None] * band_index[None, :], NE) * (2.0 * math.pi / NE)
    back_re, back_im = np.cos(back_phase), np.sin(back_phase)

    def bf(table):
        return np.ascontiguousarray(table).astype(np.float32).astype(ml_dtypes.bfloat16)

    last = SPAN // 2 * ORDER * (2.0 * math.pi / NE)
    gap = np.zeros((HALF - SPAN - 1, NE))
    freq = np.concatenate([freq_re, np.cos(last)[None] / NE, gap, freq_im, -np.sin(last)[None] / NE, gap], 0)
    kept = np.concatenate([np.arange(FOLD, SPAN), [0]])
    rest = np.zeros((NE, ROWS - FOLD - 1))
    fold_t = np.concatenate([freq_re[kept].T, rest, freq_im[kept].T, rest], 1)
    back_t = np.block([[back_re.T, back_im.T], [-back_im.T, back_re.T]])
    rows = np.concatenate([back_re, back_im], 1)
    return tuple(bf(t) for t in (freq, back_t, back_t.T, rows, fold_t))


def rows_t_table(blocks):
    rows = make_tables()[3]
    step = TS // blocks
    parts = [
        np.concatenate([rows[i * step : (i + 1) * step, :BAND].T, rows[i * step : (i + 1) * step, BAND:].T], 1)
        for i in range(blocks)
    ]
    return np.stack(parts)


def dot(left, right):
    return lax.dot_general(left, right, (((1,), (0,)), ((), ())), preferred_element_type=F32)


def dot_nt(left, right):
    return lax.dot_general(left, right, (((1,), (1,)), ((), ())), preferred_element_type=F32)


def where_am_i():
    columns = lax.axis_size("tile") // GRID_ROWS
    tile = lax.axis_index("tile")
    row = tile // columns
    k = lax.axis_index("src")
    second = k // 2 % 2 == 1
    return k, row % 2 == 1, tile % 2 == 1, (row > 0) & (row < GRID_ROWS - 1), second


def fetch_all(pairs, sems):
    copies = [pltpu.make_async_copy(source, held, sems.at[n]) for n, (source, held) in enumerate(pairs)]
    for copy in copies:
        copy.start()
    return copies


def wait_all(copies):
    for copy in copies:
        copy.wait()


def edge_kernel(
    shifts, weights, mask_at, vert_out, side_1, side_2, info_out, top, bottom, left, right, sems
):
    k, row_odd, col_odd, _inner, second = where_am_i()
    wide = 2 * HALO
    copies = fetch_all(
        (
            (mask_at.at[0, pl.ds(0, HALO), :], top),
            (mask_at.at[0, pl.ds(TS - HALO, HALO), :], bottom),
            (mask_at.at[0, :, pl.ds(0, wide)], left),
            (mask_at.at[0, :, pl.ds(TS - wide, wide)], right),
        ),
        sems,
    )
    own = shifts.shape[1]
    high, low = split(weights[...])
    rest = weights[...] - high.astype(F32)
    mid, low = split(rest)
    parts = [shifts[:1].astype(F32), shifts[1:].astype(F32), high.astype(F32), mid.astype(F32), low.astype(F32)]
    wide_parts = [jnp.concatenate([part, jnp.zeros((1, 128 - own), F32)], 1) for part in parts]
    line = sum(wide_part if n == 0 else pltpu.roll(wide_part, n * own, 1) for n, wide_part in enumerate(wide_parts))
    row = lax.broadcasted_iota(jnp.int32, (16, 128), 0)
    info = jnp.where(row == k, line, 0.0).astype(BF)
    info_out[...] = jnp.concatenate([info, jnp.zeros((16, TS - 128), BF)], 1)
    vert_out[HALO:] = info_out[...]
    wait_all(copies)
    vert_out[:HALO] = jnp.where(row_odd ^ second, top[...], bottom[...]).astype(BF)
    half = TS // 2
    first = lax.broadcasted_iota(jnp.int32, (half, wide), 1) < HALO
    before = jnp.where(first, left[:half], pltpu.roll(left[half:], HALO, 1))
    after = jnp.where(first, pltpu.roll(right[:half], HALO, 1), right[half:])
    side_1[...] = jnp.where(col_odd, before, after).astype(BF)
    side_2[...] = jnp.where(col_odd, after, before).astype(BF)


def corner_kernel(mine, theirs, side_1, side_2, send_1, send_2, info_out):
    _k, _row_odd, col_odd, _inner, _second = where_am_i()
    wide = 2 * HALO
    half = TS // 2
    ends = (slice(0, wide), slice(TS - wide, TS))
    send_1[:half] = side_1[...]
    send_2[:half] = side_2[...]
    first = lax.broadcasted_iota(jnp.int32, (HALO, wide), 1) < HALO

    def above_below(m):
        return arrived(mine[:HALO, ends[m]], theirs[:HALO, ends[m]])

    info = mine[HALO:, :wide].astype(F32) + theirs[HALO:, :wide].astype(F32)
    info_out[...] = info[:8]
    send_1[NE // 2 :] = info.astype(BF)
    above, below = above_below(0)
    before = jnp.where(first, above, pltpu.roll(below, HALO, 1))
    above, below = above_below(1)
    after = jnp.where(first, pltpu.roll(above, HALO, 1), below)
    send_1[half : NE // 2] = jnp.where(col_odd, before, after).astype(BF)
    send_2[half:] = jnp.where(col_odd, after, before).astype(BF)


def source_kernel(
    info, mine, theirs, side_1, side_2,
    mask_at, target_at, pupil_at, freq_at, back_t_at, back_at, rows_at, rows_t_at,
    dspec_out, resist_out,
    spec, amps_a, amps_b, fields, image, dspec, terms,
    mask, freq, back_t, back, own_rows, rows_turned, pupil, bits, sems,
):
    step = resist_out.shape[0]
    k, row_odd, col_odd, _inner, second = where_am_i()
    own = pl.ds(pl.multiple_of(k * step, step), step)
    copies = fetch_all(
        (
            (freq_at, freq), (mask_at.at[0], mask), (pupil_at, pupil),
            (rows_at.at[own, :], own_rows), (back_t_at, back_t), (target_at.at[0, own, :], bits),
            (back_at, back), (rows_t_at.at[k], rows_turned),
        ),
        sems,
    )
    image[...] = jnp.zeros_like(image)
    dspec[...] = jnp.zeros_like(dspec)
    terms[...] = jnp.zeros_like(terms)
    wait_all(copies[:2])

    halo_rows = jnp.concatenate(arrived(mine[:HALO], theirs[:HALO]), 0).astype(BF)
    s1, s2 = side_1[: NE // 2].astype(F32), side_2[...].astype(F32)
    left, right = jnp.where(col_odd, s1, s2), jnp.where(col_odd, s2, s1)
    first = lax.broadcasted_iota(jnp.int32, left.shape, 1) < HALO
    one = jnp.where(first, left, pltpu.roll(right, HALO, 1)).astype(BF)
    two = jnp.where(first, pltpu.roll(left, HALO, 1), right).astype(BF)
    half = TS // 2
    halo_cols = jnp.concatenate([one[:half], two[:half], one[half:], two[half:]], 0)
    prod_mid = dot(freq[:, :TS], mask[...].astype(BF)) + dot(freq[:, TS:], halo_rows)
    prod_side = dot(freq[...], halo_cols)
    prod = jnp.concatenate([prod_mid, prod_side], 1).astype(BF)
    both = dot_nt(prod, freq[...])
    spec_re = both[:SPAN, :HALF] - both[HALF : HALF + SPAN, HALF:]
    spec_im = both[:SPAN, HALF:] + both[HALF : HALF + SPAN, :HALF]
    whole = jnp.concatenate([spec_re, spec_im], 1)
    for j in range(4):
        spec[j] = whole[:, j * 128 : (j + 1) * 128]

    wait_all(copies[2:5])
    gain = pupil[...].astype(F32).astype(BF)
    sources = info.shape[0] * 8

    def where_of(s):
        group, lane = s // 8, s % 8
        down, over = info[group, lane].astype(jnp.int32), info[group, lane + 8].astype(jnp.int32)
        w = (info[group, lane + 16] + info[group, lane + 24]) + info[group, lane + 32]
        return SHIFT_MAX - down, SHIFT_MAX - over, w

    def rows_of(i, u=0, count=BATCH):
        return pl.ds(pl.multiple_of(i * (BATCH * step) + u * step, step), count * step)

    def amplitudes(i, amps):
        for u in range(BATCH):
            down, over, _w = where_of(i * BATCH + u)
            turn = lax.bitwise_and(HALF - over, HALF - 1)
            band = [spec[j, pl.ds(down, BAND), :].astype(BF) for j in range(4)]
            win_re = pltpu.roll(jnp.concatenate(band[:2], 1), turn, 1)[:, :BAND] * gain
            win_im = pltpu.roll(jnp.concatenate(band[2:], 1), turn, 1)[:, :BAND] * gain
            window = jnp.concatenate(
                [jnp.concatenate([win_re, win_im], 1), jnp.concatenate([-win_im, win_re], 1)], 0
            )
            amps[u * step : (u + 1) * step, :] = dot(own_rows[...], window).astype(BF)

    def forward(i, amps):
        for c in range(0, TS, CHUNK):
            field_re = dot(amps[...], back_t[:, c : c + CHUNK])
            field_im = dot(amps[...], back_t[:, TS + c : TS + c + CHUNK])
            fields[rows_of(i), c : c + CHUNK] = field_re
            fields[rows_of(i), TS + c : TS + c + CHUNK] = field_im
            total = image[:, c : c + CHUNK]
            for u in range(BATCH):
                _d, _o, w = where_of(i * BATCH + u)
                re, im = field_re[u * step : (u + 1) * step], field_im[u * step : (u + 1) * step]
                total = total + w * (re * re + im * im)
            image[:, c : c + CHUNK] = total

    batches = sources // BATCH
    amplitudes(0, amps_a)

    def forward_pair(p, _):
        forward(2 * p, amps_a)
        amplitudes(2 * p + 1, amps_b)
        forward(2 * p + 1, amps_b)
        amplitudes(jnp.minimum(2 * p + 2, batches - 1), amps_a)
        return 0

    lax.fori_loop(0, batches // 2, forward_pair, 0)

    wait_all(copies[5:])
    resist = jax.nn.sigmoid(steepness * (image[...] * (1.0 / sources) - threshold))
    resist_out[...] = resist.astype(BF)
    image[...] = 2.0 * (resist - bits[...].astype(F32)) * resist * (1.0 - resist) * steepness

    def backward(i, damps):
        damp = jnp.zeros((BATCH * step, 2 * BAND), F32)
        for c in range(0, TS, CHUNK):
            grad = image[:, c : c + CHUNK]
            parts_re, parts_im = [], []
            for u in range(BATCH):
                s = i * BATCH + u
                _d, _o, w = where_of(s)
                re, im = fields[rows_of(i, u, 1), c : c + CHUNK], fields[rows_of(i, u, 1), TS + c : TS + c + CHUNK]
                term = jnp.sum((grad * (re * re + im * im)).reshape(step // 8, 8, CHUNK), 0)
                terms[s] += sum(term[:, n : n + 128] for n in range(0, CHUNK, 128))
                coef = (2.0 * w / sources) * grad
                parts_re.append((coef * re).astype(BF))
                parts_im.append((coef * im).astype(BF))
            damp = damp + dot(jnp.concatenate(parts_re, 0), back[c : c + CHUNK, :])
            damp = damp + dot(jnp.concatenate(parts_im, 0), back[TS + c : TS + c + CHUNK, :])
        damps[...] = damp.astype(BF)

    empty = jnp.zeros((step, HALF - BAND), BF)
    wide_gain = jnp.concatenate([gain, jnp.zeros((BAND, HALF - BAND), BF)], 1)

    def windows(i, damps):
        for u in range(BATCH):
            down, over, _w = where_of(i * BATCH + u)
            damp = damps[u * step : (u + 1) * step, :]
            damp_re = pltpu.roll(jnp.concatenate([damp[:, :BAND], empty], 1), over, 1)
            damp_im = pltpu.roll(jnp.concatenate([damp[:, BAND:], empty], 1), over, 1)
            inside = pltpu.roll(wide_gain, over, 1).astype(F32)
            pair = jnp.concatenate(
                [jnp.concatenate([damp_re, damp_im], 1), jnp.concatenate([damp_im, -damp_re], 1)], 0
            )
            dwin = dot(rows_turned[...], pair)
            for j in range(4):
                lanes = slice(j % 2 * 128, j % 2 * 128 + 128)
                dspec[u % 2 * 4 + j, pl.ds(down, BAND), :] += dwin[:, j * 128 : (j + 1) * 128] * inside[:, lanes]

    backward(0, amps_a)

    def backward_pair(p, _):
        backward(2 * p + 1, amps_b)
        windows(2 * p, amps_a)
        backward(2 * p + 2, amps_a)
        windows(2 * p + 1, amps_b)
        return 0

    lax.fori_loop(0, batches // 2 - 1, backward_pair, 0)
    backward(batches - 1, amps_b)
    windows(batches - 2, amps_a)
    windows(batches - 1, amps_b)

    whole = jnp.concatenate([dspec[j] + dspec[4 + j] for j in range(4)], 1)
    high, low = split(whole[:FOLD])
    both = jnp.concatenate([high, low], 0)
    turn_cols = (
        lax.broadcasted_iota(jnp.int32, (HALF, HALF), 0) + lax.broadcasted_iota(jnp.int32, (HALF, HALF), 1) == SPAN
    ).astype(BF)
    turned = jnp.concatenate([dot(both[:, :HALF], turn_cols), dot(both[:, HALF:], turn_cols)], 1).astype(BF)
    at_row = lax.broadcasted_iota(jnp.int32, (FOLD, 2 * FOLD), 0)
    at_col = lax.broadcasted_iota(jnp.int32, (FOLD, 2 * FOLD), 1)
    turn_rows = (
        ((at_row + at_col == FOLD) & (at_col < FOLD)) | ((at_row + at_col == 2 * FOLD) & (at_col > FOLD))
    ).astype(BF)
    folded = dot(turn_rows, turned)
    sign = jnp.where(lax.broadcasted_iota(jnp.int32, (FOLD, 2 * HALF), 1) < HALF, 1.0, -1.0)
    dspec_out[:FOLD] = (whole[FOLD:] + sign * folded).astype(BF)
    sums = lax.dot_general(
        jnp.ones((8, 128), F32), jnp.sum(terms[...], 1), (((1,), (1,)), ((), ())),
        precision=lax.Precision.HIGHEST, preferred_element_type=F32,
    )
    dspec_out[FOLD:] = weight_rows(jnp.concatenate([whole[:8], jnp.zeros_like(whole[:8])], 0), sums[:1])


def weight_rows(line, sums):
    high = sums.astype(BF).astype(F32)
    mid = (sums - high).astype(BF).astype(F32)
    low = sums - high - mid
    row = lax.broadcasted_iota(jnp.int32, line.shape, 0)
    kept = jnp.where(row == 0, line, 0.0)
    for n, piece in enumerate((high, mid, low)):
        if line.shape[1] > 128:
            piece = jnp.concatenate([piece, jnp.zeros((1, line.shape[1] - 128), F32)], 1)
        kept = jnp.where(row == n + 1, piece, kept)
    return kept.astype(BF)


def weight_sums(rows):
    return rows[1:2] + rows[2:3] + rows[3:4]


def add(*parts):
    parts = [part.astype(F32) for part in parts]
    rows = [weight_sums(part[FOLD:]) for part in parts]
    sums = (rows[0] + rows[1]) + (rows[2] + rows[3])
    total = (parts[0] + parts[1]) + (parts[2] + parts[3])
    high = lax.reduce_precision(sums, 8, 7)
    mid = lax.reduce_precision(sums - high, 8, 7)
    row = lax.broadcasted_iota(jnp.int32, total.shape, 0) - FOLD
    for n, piece in enumerate((high, mid, sums - high - mid)):
        total = jnp.where(row == n + 1, piece, total)
    return total.astype(BF)


def split(values):
    high = values.astype(BF)
    return high, (values - high.astype(F32)).astype(BF)


def pack_sides(before, after, col_odd, side_1, side_2):
    side_1[...] = jnp.where(col_odd, before, after).astype(BF)
    side_2[...] = jnp.where(col_odd, after, before).astype(BF)


def mask_kernel(mask, part_1, part_2, freq, fold_t, base_out, rims_out, side_1, side_2):
    _k, _row_odd, col_odd, _inner, _second = where_am_i()
    total = part_1[...].astype(F32) + part_2[...].astype(F32)
    swapped = jnp.concatenate([total[:, HALF:], -total[:, :HALF]], 1)
    both = dot(jnp.concatenate([*split(total), *split(swapped)], 0), freq[...])
    prod = jnp.concatenate([both[:ROWS] + both[ROWS : 2 * ROWS], both[2 * ROWS : 3 * ROWS] + both[3 * ROWS :]], 0)
    high, low = split(prod)
    ext = dot(fold_t[...], high) + dot(fold_t[...], low)
    base_out[...] = mask[0] - mask_rate * ext[:TS, :TS]
    rims_out[...] = ext[TS:, :TS]
    sides = ext[:, TS:]
    half, quarter = TS // 2, HALO
    upper = jnp.concatenate([sides[:half], sides[TS : TS + quarter]], 0)
    lower = jnp.concatenate([sides[half:TS], sides[TS + quarter :]], 0)
    first = lax.broadcasted_iota(jnp.int32, upper.shape, 1) < HALO
    before = jnp.where(first, upper, pltpu.roll(lower, HALO, 1))
    after = jnp.where(first, pltpu.roll(upper, HALO, 1), lower)
    pack_sides(before, after, col_odd, side_1, side_2)


def arrived(mine, theirs):
    mine, theirs = mine.astype(F32), theirs.astype(F32)
    _k, row_odd, _col_odd, inner, second = where_am_i()
    g1 = jnp.where(second, theirs, mine)
    g2 = jnp.where(inner, jnp.where(second, mine, theirs), 0.0)
    return jnp.where(row_odd, g1, g2), jnp.where(row_odd, g2, g1)


def from_sides(side_1, side_2):
    _k, _row_odd, col_odd, _inner, _second = where_am_i()
    s1, s2 = side_1.astype(F32), side_2.astype(F32)
    before, after = jnp.where(col_odd, s1, s2), jnp.where(col_odd, s2, s1)
    first = lax.broadcasted_iota(jnp.int32, before.shape, 1) < HALO
    left = jnp.where(first, before, 0.0), jnp.where(first, pltpu.roll(before, HALO, 1), 0.0)
    right = jnp.where(first, 0.0, pltpu.roll(after, HALO, 1)), jnp.where(first, 0.0, after)
    return left, right


def rim_kernel(rims_in, side_1, side_2, weight, vert_out, rims):
    _k, row_odd, _col_odd, _inner, second = where_am_i()
    rims[...] = rims_in[...]
    left, right = from_sides(side_1[TS // 2 :], side_2[TS // 2 :])
    wide = 2 * HALO
    for n in range(2):
        rows = slice(n * HALO, (n + 1) * HALO)
        rims[rows, :wide] += left[n]
        rims[rows, TS - wide :] += right[n]
    vert_out[:HALO] = jnp.where(row_odd ^ second, rims[:HALO], rims[HALO:]).astype(BF)
    vert_out[HALO:] = weight_rows(jnp.zeros((16, TS), F32), weight[:1])


def final_kernel(
    base_in, side_1, side_2, mine, theirs, weight, other, near, far, source_weights,
    mask_at, resist_at, weights_out, base, resist, sems,
):
    k, _row_odd, _col_odd, _inner, second = where_am_i()
    step = near.shape[0] // 4
    half = TS // 2
    for m in range(8):
        piece = (near, far)[m % 2][m // 2 * step : (m // 2 + 1) * step, :]
        at = lax.bitwise_xor(k, m)
        resist[pl.ds(pl.multiple_of(at * step, step), step), :] = piece.astype(F32)
    resist_done = pltpu.make_async_copy(resist, resist_at.at[0], sems.at[0])
    resist_done.start()
    base[...] = base_in[...]
    left, right = from_sides(side_1[:half], side_2[:half])
    wide = 2 * HALO
    for n in range(2):
        rows = slice(n * half, (n + 1) * half)
        base[rows, :wide] -= mask_rate * left[n]
        base[rows, TS - wide :] -= mask_rate * right[n]
    above, below = arrived(mine[:HALO], theirs[:HALO])
    base[:HALO] -= mask_rate * above
    base[TS - HALO :] -= mask_rate * below
    mask_done = pltpu.make_async_copy(base, mask_at.at[0], sems.at[1])
    mask_done.start()
    from_1, from_2 = weight_sums(mine[HALO:, :128].astype(F32)), weight_sums(theirs[HALO:, :128].astype(F32))
    from_1, from_2 = jnp.where(second, from_2, from_1), jnp.where(second, from_1, from_2)
    total = (weight[:1] + from_1) + (from_2 + other[:1])
    own = source_weights.shape[1]
    total = pltpu.roll(jnp.broadcast_to(total, (8, 128)), lax.bitwise_and(128 - own * k, 127), 1)
    tiles = lax.axis_size("tile")
    weights_out[...] = source_weights[...] - source_rate * total[:1, :own] / (TS * TS * tiles)
    mask_done.wait()
    resist_done.wait()


SMEM = pl.BlockSpec(memory_space=pltpu.SMEM)
VMEM = pl.BlockSpec(memory_space=pltpu.VMEM)
HBM = pl.BlockSpec(memory_space=pl.ANY)


def shaped(shape, dtype):
    return jax.ShapeDtypeStruct(shape, dtype)


def grid_routes(tiles, columns):
    row_swap = [(t, t ^ columns) for t in range(tiles)]
    row_next = [(t, t + columns) for t in range(tiles) if (t // columns) % 2 == 1 and t + columns < tiles]
    col_swap = [(t, t ^ 1) for t in range(tiles)]
    col_next = [(t, t + 1) for t in range(tiles) if t % 2 == 1 and (t + 1) % columns != 0]
    back = lambda route: route + [(b, a) for a, b in route]
    return row_swap, back(row_next), col_swap, back(col_next)


def route_of(first, second, groups, distance=0):
    return [
        (a * groups + k, b * groups + (k ^ distance)) for k in range(groups) for a, b in (second if k // 2 % 2 == 1 else first)
    ]


def src_swap(block, distance, count):
    return lax.ppermute(block, "src", [(i, i ^ distance) for i in range(count)])


def tile_swap(block, distance, count):
    return lax.ppermute(block, "tile", [(i, i ^ distance) for i in range(count)])


def per_device(mask, target, shifts, source_weights, pupil):
    tiles, groups = lax.axis_size("tile"), lax.axis_size("src")
    columns = tiles // GRID_ROWS
    k = lax.axis_index("src")
    row_swap, row_next, col_swap, col_next = grid_routes(tiles, columns)
    row_ring = row_next + [(t, t ^ (3 * columns)) for t in range(tiles) if (t // columns) % 3 == 0]
    freq, back_t, back, rows, fold_t = (jnp.asarray(t) for t in make_tables())
    rows_t = jnp.asarray(rows_t_table(groups))
    own = shifts.shape[0]
    step = TS // groups

    vert, side_1, side_2, info = pl.pallas_call(
        edge_kernel,
        out_shape=(shaped((HALO + 16, TS), BF),) + (shaped((TS // 2, 128), BF),) * 2 + (shaped((16, TS), BF),),
        in_specs=[VMEM] * 2 + [HBM],
        out_specs=(VMEM,) * 4,
        scratch_shapes=[pltpu.VMEM((HALO, TS), F32)] * 2
        + [pltpu.VMEM((TS, 2 * HALO), F32)] * 2
        + [pltpu.SemaphoreType.DMA((4,))],
        name="edges",
    )(shifts.T, source_weights[None], mask)
    mine = lax.ppermute(vert, ("tile", "src"), route_of(row_swap, row_ring, groups, 4))
    mine = jnp.concatenate([mine[:HALO], mine[HALO:] + info], 0)
    theirs = src_swap(mine, 2, groups)
    side_1, side_2, info = pl.pallas_call(
        corner_kernel,
        out_shape=(shaped((NE // 2 + 16, 128), BF), shaped((NE // 2, 128), BF), shaped((8, 128), F32)),
        in_specs=[VMEM] * 4,
        out_specs=(VMEM,) * 3,
        name="corners",
    )(mine, theirs, side_1, side_2)
    side_1 = lax.ppermute(side_1, ("tile", "src"), route_of(col_swap, col_swap, groups, 1))
    side_2 = lax.ppermute(side_2, "tile", col_next)
    info = info + side_1[NE // 2 : NE // 2 + 8].astype(F32)

    part, resist = pl.pallas_call(
        source_kernel,
        out_shape=(shaped((ROWS, 2 * HALF), BF), shaped((step, TS), BF)),
        in_specs=[SMEM] + [VMEM] * 4 + [HBM] * 8,
        out_specs=(VMEM, VMEM),
        scratch_shapes=[
            pltpu.VMEM((4, SPAN, 128), F32),
            pltpu.VMEM((BATCH * step, 2 * BAND), BF),
            pltpu.VMEM((BATCH * step, 2 * BAND), BF),
            pltpu.VMEM((groups * own * step, 2 * TS), F32),
            pltpu.VMEM((step, TS), F32),
            pltpu.VMEM((8, SPAN, 128), F32),
            pltpu.VMEM((128, 8, 128), F32),
            pltpu.VMEM((TS, TS), F32),
            pltpu.VMEM((2 * HALF, NE), BF),
            pltpu.VMEM((2 * BAND, 2 * TS), BF),
            pltpu.VMEM((2 * TS, 2 * BAND), BF),
            pltpu.VMEM((step, 2 * BAND), BF),
            pltpu.VMEM((BAND, 2 * step), BF),
            pltpu.VMEM((BAND, BAND), jnp.int32),
            pltpu.VMEM((step, TS), jnp.int32),
            pltpu.SemaphoreType.DMA((8,)),
        ],
        compiler_params=pltpu.CompilerParams(vmem_limit_bytes=60 << 20),
        name="sources",
    )(
        info, mine, theirs, side_1, side_2, mask, target, pupil,
        freq, back_t, back, rows, rows_t,
    )

    near = src_swap(resist, 2, groups)
    part = add(part, *(src_swap(part, distance, groups) for distance in (2, 4, 6)))
    other = src_swap(part, 1, groups)
    weight = weight_sums(part[FOLD:, :128].astype(F32)) + weight_sums(other[FOLD:, :128].astype(F32))
    weight = jnp.broadcast_to(weight, (8, 128))
    weight = weight + tile_swap(weight, 1, tiles)
    base, rims, side_1, side_2 = pl.pallas_call(
        mask_kernel,
        out_shape=(shaped((TS, TS), F32), shaped((2 * HALO, TS), F32)) + (shaped((NE // 2, 128), BF),) * 2,
        in_specs=[VMEM] * 5,
        out_specs=(VMEM,) * 4,
        compiler_params=pltpu.CompilerParams(vmem_limit_bytes=40 << 20),
        name="mask_gradient",
    )(mask, part, other, freq, fold_t)

    near = jnp.concatenate([resist, near], 0)
    side_1, side_2, weight, near = lax.optimization_barrier((side_1, side_2, weight, near))
    far = src_swap(near, 4, groups)
    side_1 = lax.ppermute(side_1, "tile", col_swap)
    side_2 = lax.ppermute(side_2, "tile", col_next)
    weight = (weight + tile_swap(weight, 2, tiles)) + (tile_swap(weight, 4, tiles) + tile_swap(weight, 6, tiles))
    side_1, side_2, weight, far = lax.optimization_barrier((side_1, side_2, weight, far))
    rim = pl.pallas_call(
        rim_kernel,
        out_shape=shaped((HALO + 16, TS), BF),
        in_specs=[VMEM] * 4,
        out_specs=VMEM,
        scratch_shapes=[pltpu.VMEM((2 * HALO, TS), F32)],
        name="row_rims",
    )(rims, side_1, side_2, weight)
    near = jnp.concatenate([near, far], 0)
    rim, weight, near = lax.optimization_barrier((rim, weight, near))
    mine = lax.ppermute(rim, ("tile", "src"), route_of(row_swap, row_ring, groups))
    other = tile_swap(weight, 2 * columns, tiles)
    far = src_swap(near, 1, groups)
    theirs = src_swap(mine, 2, groups)
    new_mask, resist_tile, new_weights = pl.pallas_call(
        final_kernel,
        out_shape=(shaped((1, TS, TS), F32),) * 2 + (shaped((1, own), F32),),
        in_specs=[VMEM] * 10,
        out_specs=(HBM, HBM, VMEM),
        scratch_shapes=[
            pltpu.VMEM((TS, TS), F32),
            pltpu.VMEM((TS, TS), F32),
            pltpu.SemaphoreType.DMA((2,)),
        ],
        compiler_params=pltpu.CompilerParams(vmem_limit_bytes=24 << 20),
        name="new_mask",
    )(base, side_1, side_2, mine, theirs, weight, other, near, far, source_weights[None])

    return (new_mask, new_weights[0], resist_tile)


def solution(mesh):
    in_specs = (P("tile", None, None), P("tile", None, None), P("src", None), P("src"), P())
    out_specs = (P("tile", None, None), P("src"), P("tile", None, None))
    return jax.shard_map(
        per_device, mesh=mesh, in_specs=in_specs, out_specs=out_specs, check_vma=False
    )
```
